256 devices in a mesh: stream: 32 (over y, x, core), span: 8 (over z).
Axes of the slice: x: 4, y: 4, z: 8, core: 2. Of those that a mesh axis runs over, the one named last changes fastest.
Arguments:
- solution: float32 [512, 128, 128], P('stream', 'span'), may hold values from -6 to 6
- residual: float32 [512, 128, 128], P('stream', 'span'), may hold values from -6 to 6
- direction: float32 [512, 128, 128], P('stream', 'span'), may hold values from -6 to 6
- rz_old: float32 [1], replicated, may hold values from 838860.8 to 3355443.2
- wall_flags: int32 [2, 512, 128], P(None, 'stream', 'span'), may hold values 0 or 1
- owner_list: int32 [256], P(('stream', 'span')), may hold values from 0 to 15
- coarse_basis: bfloat16 [64, 512, 128, 128], P(None, 'stream', 'span'), may hold values from -0.09375 to 0.09375
- coarse_inverse: float32 [1024, 1024], replicated, as said below
Outputs:
- new_solution: float32 [512, 128, 128], P('stream', 'span')
- new_residual: float32 [512, 128, 128], P('stream', 'span')
- new_direction: float32 [512, 128, 128], P('stream', 'span')
The draws below stay inside these ranges and needn't reach their ends.
Inputs may be any that keep to these rules, and one draw needn't show every extreme that they name: `coarse_inverse`: symmetric positive definite.
All inputs are finite; a program needn't handle non-finite values. No bound on the sum of `wall_flags` on one device may be relied on, other than what follows from the above.
Results may differ from the reference program's by a relative error of at most 0.0015.
The reference program's roundings to bfloat16 on the way (of `coarse_low`) count: a program that leaves them out, or rounds other values in their place, can miss the bound.
Values sent between devices are 32-bit elements; how exact they have to be, the bound alone decides.
A program may use at most 64 MiB of HBM per device.

```python
import math
import jax
import jax.numpy as jnp
import numpy as np
from jax import lax

CX = 16
CY = 16
CZ = 128
NB = 64
CO = 16
NX = 512
NY = 128
NZ = 128
SUBS = 256
N_STREAM = 32
N_SPAN = 8


def draw_coarse_inverse(key, part):
    key = jax.random.fold_in(key, 5)
    key_off, key_diag = jax.random.split(key)
    order = CO * NB
    raw = jax.random.uniform(key_off, (order, order), jnp.float32, -1.0, 1.0)
    symmetric = (raw + raw.T) * (0.5 * 2.9 / order)
    diag_vals = jnp.exp(jax.random.uniform(key_diag, (order,), jnp.float32, jnp.log(3.0), jnp.log(8.0)))
    identity = jnp.eye(order, dtype=jnp.float32)
    return symmetric * (1.0 - identity) + identity * diag_vals[None, :]


def plant(result, key, smallest, largest):
    extent = result.shape
    place = [jax.random.randint(jax.random.fold_in(key, axis), (), 0, extent[axis]) for axis in range(len(extent))]
    result = result.at[tuple(place)].set(smallest)
    longest = extent.index(max(extent))
    place[longest] = (place[longest] + 1) % extent[longest]
    return result.at[tuple(place)].set(largest)


def steps_of(rng, extent, shards, low, high):
    def one(axis_at, shards_of):
        steps = jax.random.uniform(jax.random.fold_in(jax.random.fold_in(rng, 6), axis_at), (shards_of,), jnp.float32, low / len(shards), high / len(shards))
        return jnp.repeat(jnp.exp(steps), extent[axis_at] // shards_of).reshape((-1,) + (1,) * (len(extent) - axis_at - 1))

    loudness = one(*shards[0])
    for cut in shards[1:]:
        loudness = loudness * one(*cut)
    return loudness


def cumulative_ranks(amount, skew):
    weights = [(1 << 20) // math.isqrt(grade ** skew) + 1 for grade in range(1, amount + 1)]
    deviation = 1 + sum(weights) // (1 << 30)
    return np.cumsum(np.array([max(1, weight // deviation) for weight in weights]))


def skewed_ids(own_key, dims, number_of, skew):
    listing = cumulative_ranks(number_of, skew)
    lot = jax.random.randint(jax.random.fold_in(own_key, 1), dims, 0, int(listing[number_of - 1]))
    standing = jnp.searchsorted(jnp.asarray(listing, jnp.int32), lot, side="right")
    return jax.random.permutation(jax.random.fold_in(own_key, 2), number_of)[standing].astype(jnp.int32)


def gaussian(stream_key, shape, deviation, limit, pieces=(), kind=jnp.bfloat16):
    drawn = jax.random.normal(stream_key, shape, jnp.float32) * deviation
    if len(pieces) > 0:
        drawn = steps_of(stream_key, shape, pieces, -0.22, 0.18) * drawn
    return jnp.clip(drawn, min=-limit, max=limit).astype(kind)


def setup_inputs(seed: int = 0) -> dict:
    seeds = jax.random.split(jax.random.key(seed), 9)
    solution = gaussian(seeds[0], (NX, NY, NZ), 1.0, 6.0, ((0, 32), (1, 8)), jnp.float32)
    residual = gaussian(seeds[1], (NX, NY, NZ), 1.0, 6.0, ((0, 32), (1, 8)), jnp.float32)
    direction = gaussian(seeds[2], (NX, NY, NZ), 1.0, 6.0, ((0, 32), (1, 8)), jnp.float32)
    rz_old = jnp.clip(jnp.exp(jax.random.uniform(seeds[3], (1,), jnp.float32, math.log(838860.8), math.log(3355443.2))), 838860.8, 3355443.2)
    wall_flags = plant((jax.random.randint(seeds[4], (2, NX, NY), 0, 2) < 1).astype(jnp.int32), jax.random.fold_in(seeds[4], 1), 0, 1)
    owner_list = plant(skewed_ids(seeds[5], (SUBS,), CO, 2), jax.random.fold_in(seeds[5], 3), 0, CO - 1).astype(jnp.int32)
    coarse_basis = gaussian(seeds[6], (NB, NX, NY, NZ), (CX * CY * CZ // 8) ** -0.5, 0.09375, ((1, 32), (2, 8)))
    coarse_inverse = draw_coarse_inverse(jax.random.fold_in(seeds[8], 71), 0)
    return {"solution": solution, "residual": residual, "direction": direction, "rz_old": rz_old, "wall_flags": wall_flags, "owner_list": owner_list, "coarse_basis": coarse_basis, "coarse_inverse": coarse_inverse}


def apply_operator(field, wall_flags):
    neighbor_sum = jnp.roll(field, 1, 0) + jnp.roll(field, -1, 0)
    span_padded = jnp.pad(field, ((0, 0), (1, 1), (0, 0)))
    neighbor_sum = neighbor_sum + span_padded[:, 2:] + span_padded[:, :-2]
    low_keep = (1 - wall_flags[0]).astype(jnp.float32)[:, :, None]
    top_keep = (1 - wall_flags[1]).astype(jnp.float32)[:, :, None]
    z_padded = jnp.concatenate([field[:, :, :1] * low_keep, field, field[:, :, -1:] * top_keep], 2)
    neighbor_sum = neighbor_sum + z_padded[:, :, 2:] + z_padded[:, :, :-2]
    return 6.0 * field - neighbor_sum


def diagonal_of(wall_flags, depth):
    low_keep = (1 - wall_flags[0]).astype(jnp.float32)
    top_keep = (1 - wall_flags[1]).astype(jnp.float32)
    level = jnp.arange(depth)
    low_mask = (level == 0).astype(jnp.float32)
    top_mask = (level == depth - 1).astype(jnp.float32)
    return 6.0 - low_keep[:, :, None] * low_mask - top_keep[:, :, None] * top_mask


def reference(solution, residual, direction, rz_old, wall_flags, owner_list, coarse_basis, coarse_inverse):
    applied = apply_operator(direction, wall_flags)
    curvature = jnp.sum(direction * applied)
    step_size = rz_old[0] / curvature
    new_solution = solution + step_size * direction
    new_residual = residual - step_size * applied
    residual_low = residual.astype(jnp.bfloat16)
    applied_low = applied.astype(jnp.bfloat16)

    def project(slab_index):
        start = (slab_index * CX).astype(jnp.int32)
        basis_slab = lax.dynamic_slice_in_dim(coarse_basis, start, CX, 1).astype(jnp.float32)
        basis_slab = basis_slab.reshape(NB, CX, N_SPAN, CY, NZ)
        res_slab = lax.dynamic_slice_in_dim(residual_low, start, CX, 0).astype(jnp.float32).reshape(CX, N_SPAN, CY, NZ)
        app_slab = lax.dynamic_slice_in_dim(applied_low, start, CX, 0).astype(jnp.float32).reshape(CX, N_SPAN, CY, NZ)
        first = jnp.einsum('bxpyz,xpyz->pb', basis_slab, res_slab)
        second = jnp.einsum('bxpyz,xpyz->pb', basis_slab, app_slab)
        return first - step_size * second

    coarse_res = lax.map(project, jnp.arange(N_STREAM, dtype=jnp.int32)).reshape(N_STREAM * N_SPAN, NB)
    selector = (owner_list[:, None] == jnp.arange(CO, dtype=jnp.int32)[None, :]).astype(jnp.float32)
    coarse_rhs = jnp.dot(selector.T, coarse_res, precision=lax.Precision.HIGHEST)
    coarse_sol = jnp.dot(coarse_inverse, coarse_rhs.reshape(CO * NB), precision=lax.Precision.HIGHEST).reshape(CO, NB)
    coarse_low = coarse_sol[owner_list].astype(jnp.bfloat16).reshape(N_STREAM, N_SPAN, NB)

    def extend(slab_index):
        start = (slab_index * CX).astype(jnp.int32)
        basis_slab = lax.dynamic_slice_in_dim(coarse_basis, start, CX, 1).astype(jnp.float32)
        basis_slab = basis_slab.reshape(NB, CX, N_SPAN, CY, NZ)
        weights = coarse_low[slab_index].astype(jnp.float32)
        return jnp.einsum('pb,bxpyz->xpyz', weights, basis_slab).reshape(CX, NY, NZ)

    correction = lax.map(extend, jnp.arange(N_STREAM, dtype=jnp.int32)).reshape(NX, NY, NZ)
    precond = new_residual / diagonal_of(wall_flags, NZ) + correction
    rz_new = jnp.sum(new_residual * precond)
    new_direction = precond + (rz_new / rz_old[0]) * direction
    return new_solution, new_residual, new_direction
```

```python
import jax
import jax.numpy as jnp
from jax import lax
from jax.experimental import pallas as pl
from jax.experimental.pallas import tpu as pltpu
from jax.sharding import PartitionSpec as P

MESH = pl.DeviceIdType.MESH
F32 = jnp.float32
BF16 = jnp.bfloat16
NT = (((1,), (1,)), ((), ()))


def iota(shape, dim):
    return lax.broadcasted_iota(jnp.int32, shape, dim)


def split3(value):
    first = value.astype(BF16)
    rest = value - first.astype(F32)
    second = rest.astype(BF16)
    third = (rest - second.astype(F32)).astype(BF16)
    return first, second, third


def places():
    stream, z = lax.axis_index("stream"), lax.axis_index("span")
    y, x, core = stream // 8, lax.rem(stream // 2, 4), lax.rem(stream, 2)
    halo = [
        (lax.rem(stream + 1, 32), z),
        (lax.rem(stream + 31, 32), z),
        (stream, lax.rem(z + 1, 8)),
        (stream, lax.rem(z + 7, 8)),
    ]
    line = [
        ((y * 4 + x) * 2 + lax.rem(core + other, 2), lax.rem(z + away, 8))
        for away in (4, 3, 5, 2, 6, 1, 7, 0)
        for other in range(2)
        if away or other
    ]
    plane = [
        ((lax.rem(y + away // 4, 4) * 4 + lax.rem(x + away % 4, 4)) * 2 + core, z)
        for away in (10, 9, 11, 6, 14, 2, 8, 5, 7, 13, 15, 1, 3, 4, 12)
    ]
    return halo, line, plane, z * 2 + core, y * 4 + x, z


def kernel(
    sol_hbm, res_hbm, dir_hbm, rz_hbm, wall_hbm, own_hbm, basis_hbm, inv_hbm,
    new_sol, new_res, new_dir,
    sol, res, dirn, rz, wall, own, basis, inv,
    low_face, high_face, halo_buf, app, inv_diag, w_res, w_app, group_sum, part_res, v_ref,
    line_buf, plane_buf,
    in_sem, basis_sem, halo_send, halo_recv, line_send, line_recv, plane_send, plane_recv,
):
    halo, line, plane, line_me, plane_me, z = places()
    barrier = pltpu.get_barrier_semaphore()
    for peer in halo + line + plane:
        pl.semaphore_signal(barrier, inc=1, device_id=peer, device_id_type=MESH)
    loads = [
        pltpu.make_async_copy(src, dst, in_sem.at[i])
        for i, (src, dst) in enumerate(
            ((dir_hbm, dirn), (wall_hbm, wall), (res_hbm, res), (rz_hbm, rz), (own_hbm, own), (sol_hbm, sol), (inv_hbm, inv))
        )
    ]
    basis_loads = [
        pltpu.make_async_copy(basis_hbm.at[pl.ds(8 * i, 8)], basis.at[pl.ds(8 * i, 8)], basis_sem.at[i])
        for i in range(8)
    ]
    for load in loads[:5] + basis_loads + loads[5:]:
        load.start()

    lane = iota((16, 128), 1)
    row = iota((16, 128), 0)
    group_sum[...] = (iota((1024, 128), 0) // 16 == iota((1024, 128), 1) % 64).astype(F32).astype(BF16)

    loads[0].wait()
    for x in range(16):
        low_face[pl.ds(x, 1), :] = dirn[x, pl.ds(0, 1), :]
        high_face[pl.ds(x, 1), :] = dirn[x, pl.ds(15, 1), :]
    pl.semaphore_wait(barrier, len(halo + line + plane))
    sends = []
    for i, (src, peer) in enumerate(zip((dirn.at[15], dirn.at[0], high_face, low_face), halo)):
        copy = pltpu.make_async_remote_copy(
            src_ref=src, dst_ref=halo_buf.at[i], send_sem=halo_send.at[i], recv_sem=halo_recv.at[i],
            device_id=peer, device_id_type=MESH,
        )
        copy.start()
        sends.append(copy)

    loads[1].wait()
    loads[2].wait()
    same = iota((16, 16), 0) == iota((16, 16), 1)
    keep_low = (1 - wall[0]).astype(F32)
    keep_top = (1 - wall[1]).astype(F32)
    sum_rr = jnp.zeros((16, 128), F32)
    for x in range(16):
        own_d = dirn[x]
        low = jnp.sum(jnp.where(same, keep_low[x : x + 1, :], 0.0), axis=1, keepdims=True)
        top = jnp.sum(jnp.where(same, keep_top[x : x + 1, :], 0.0), axis=1, keepdims=True)
        around = jnp.where(lane == 0, own_d * low, pltpu.roll(own_d, 1, 1))
        around += jnp.where(lane == 127, own_d * top, pltpu.roll(own_d, 127, 1))
        around += jnp.where(row == 0, 0.0, pltpu.roll(own_d, 1, 0))
        around += jnp.where(row == 15, 0.0, pltpu.roll(own_d, 15, 0))
        if x > 0:
            around += dirn[x - 1]
        if x < 15:
            around += dirn[x + 1]
        app[x] = 6.0 * own_d - around
        diag = 6.0 - jnp.where(lane == 0, low, 0.0) - jnp.where(lane == 127, top, 0.0)
        inverse = 1.0 / diag
        inv_diag[x] = inverse
        r = res[x]
        sum_rr += r * r * inverse
        r_low = r.astype(BF16)
        w_res[0:16, 128 * x : 128 * x + 128] = r_low
        w_res[16:32, 128 * x : 128 * x + 128] = (r - r_low.astype(F32)).astype(BF16)

    pick = iota((32, 1024), 0) % 16 == iota((32, 1024), 1) % 16

    def slab(pair):
        return jnp.concatenate(
            [basis[:, 2 * pair].reshape(1024, 128), basis[:, 2 * pair + 1].reshape(1024, 128)], axis=1
        )

    def project(weights):
        total = jnp.zeros((32, 1024), F32)
        for pair in range(8):
            total += lax.dot_general(
                weights[:, 256 * pair : 256 * pair + 256], slab(pair), NT, preferred_element_type=F32
            )
        total = jnp.where(pick, total, 0.0)
        first = jnp.sum(total[0:16], axis=0, keepdims=True)
        second = jnp.sum(total[16:32], axis=0, keepdims=True)
        at = iota((8, 1024), 0)
        both = jnp.where(at == 0, first, jnp.where(at == 1, second, 0.0))
        one, two, three = (part.astype(F32) for part in split3(both))
        stacked = jnp.concatenate([one, two, three, jnp.zeros_like(one)], axis=0).astype(BF16)
        sums = jnp.dot(stacked, group_sum[...], preferred_element_type=F32)
        return sums[0:8] + sums[8:16] + sums[16:24]

    for load in basis_loads:
        load.wait()
    part_res[...] = project(w_res)

    for copy in sends:
        copy.wait_recv()
    from_low = jnp.where(z > 0, 1.0, 0.0)
    from_high = jnp.where(z < 7, 1.0, 0.0)
    sum_dq = jnp.zeros((16, 128), F32)
    sum_rq = jnp.zeros((16, 128), F32)
    sum_qq = jnp.zeros((16, 128), F32)
    for x in range(16):
        q = app[x]
        if x == 0:
            q -= halo_buf[0]
        if x == 15:
            q -= halo_buf[1]
        q -= jnp.where(row == 0, halo_buf[2, pl.ds(x, 1), :] * from_low, 0.0)
        q -= jnp.where(row == 15, halo_buf[3, pl.ds(x, 1), :] * from_high, 0.0)
        app[x] = q
        scaled = q * inv_diag[x]
        sum_dq += dirn[x] * q
        sum_rq += res[x] * scaled
        sum_qq += q * scaled
        q_low = q.astype(BF16)
        w_app[0:16, 128 * x : 128 * x + 128] = q_low
        w_app[16:32, 128 * x : 128 * x + 128] = (q - q_low.astype(F32)).astype(BF16)
    part_app = project(w_app)
    loads[4].wait()
    lane1 = lane[0:1]
    scalars = own[0].astype(F32) * jnp.where(lane1 == 4, 1.0, 0.0)
    for i, value in enumerate((sum_dq, sum_rr, sum_rq, sum_qq)):
        whole = jnp.sum(jnp.sum(value, axis=0, keepdims=True), axis=1, keepdims=True)
        scalars = jnp.where(lane1 == i, whole, scalars)
    line_buf[line_me, pl.ds(0, 1), :] = jnp.where(lane1 < 64, part_res[0:1, :], part_app[0:1, :])
    line_buf[line_me, pl.ds(1, 1), :] = jnp.where(lane1 < 64, part_res[1:2, :], part_app[1:2, :])
    line_buf[line_me, pl.ds(2, 1), :] = scalars

    copies = []
    for i, peer in enumerate(line):
        copy = pltpu.make_async_remote_copy(
            src_ref=line_buf.at[line_me], dst_ref=line_buf.at[line_me], send_sem=line_send.at[i],
            recv_sem=line_recv.at[i], device_id=peer, device_id_type=MESH,
        )
        copy.start()
        copies.append(copy)
    sends += copies
    for copy in copies:
        copy.wait_recv()
    rows = pl.ds(pl.multiple_of(plane_me * 16, 16), 16)
    for kind in range(3):
        plane_buf[kind, rows, :] = line_buf[:, kind, :]
    copies = []
    for i, peer in enumerate(plane):
        copy = pltpu.make_async_remote_copy(
            src_ref=plane_buf.at[:, rows], dst_ref=plane_buf.at[:, rows], send_sem=plane_send.at[i],
            recv_sem=plane_recv.at[i], device_id=peer, device_id_type=MESH,
        )
        copy.start()
        copies.append(copy)
    sends += copies
    loads[3].wait()
    loads[5].wait()
    loads[6].wait()
    for copy in copies:
        copy.wait_recv()

    flat = plane_buf[2]
    totals = jnp.sum(flat, axis=0, keepdims=True)
    rz_old = rz[0]
    step = rz_old / totals[:, 0:1]
    for x in range(16):
        new_sol[x] = sol[x] + step * dirn[x]
    owners = lax.dot_general(
        jnp.ones((16, 128), BF16), jnp.where(iota((256, 128), 1) == 4, flat, 0.0).astype(BF16), NT,
        preferred_element_type=F32,
    )
    at = iota((16, 256), 0)
    wanted = jnp.where(at < 8, 2 * at, 2 * at - 15).astype(F32)
    chosen = (owners == wanted).astype(F32).astype(BF16)
    sums = jnp.zeros((16, 256), F32)
    for part in split3(jnp.concatenate([plane_buf[0], plane_buf[1]], axis=1)):
        sums += jnp.dot(chosen, part, preferred_element_type=F32)
    lane8 = iota((8, 128), 1)
    row8 = iota((8, 128), 0)

    def coarse(even, odd):
        return jnp.where(
            lane8 < 64, even - step * pltpu.roll(even, 64, 1), pltpu.roll(odd, 64, 1) - step * odd
        )

    rhs = coarse(sums[0:8, 0:128], sums[8:16, 0:128])
    rhs_rest = coarse(sums[0:8, 128:256], sums[8:16, 128:256])
    v_ref[...] = rhs

    def block(tile, total):
        values = v_ref[pl.ds(tile, 1), :]
        for k in range(16):
            column = jnp.sum(jnp.where(lane8 == row8 + 8 * k, values, 0.0), axis=1, keepdims=True)
            total += column * inv[pl.ds(pl.multiple_of(tile * 128 + 8 * k, 8), 8), :]
        return total

    total = lax.fori_loop(0, 8, block, jnp.zeros((8, 1024), F32))
    answer = jnp.zeros((8, 128), F32)
    for tile in range(8):
        answer = jnp.where(
            row8 == tile, jnp.sum(total[:, 128 * tile : 128 * tile + 128], axis=0, keepdims=True), answer
        )
    answer = answer.astype(BF16).astype(F32)
    inner = jnp.sum(jnp.sum(answer * (rhs + rhs_rest), axis=0, keepdims=True), axis=1, keepdims=True)
    rz_new = totals[:, 1:2] - 2.0 * step * totals[:, 2:3] + step * step * totals[:, 3:4] + inner
    ratio = rz_new / rz_old
    mine = own[0]
    here = jnp.where(row8 == (mine >> 1), jnp.where((lane8 >> 6) == (mine & 1), answer, 0.0), 0.0)
    here = jnp.broadcast_to(jnp.sum(here, axis=0, keepdims=True), (16, 128)).astype(BF16)
    spread = lax.dot_general(here, group_sum[...], NT, preferred_element_type=F32)
    spread = jnp.where(pick[0:16], spread, 0.0).astype(BF16)
    for pair in range(8):
        correction = jnp.dot(spread, slab(pair), preferred_element_type=F32)
        for side in range(2):
            x = 2 * pair + side
            d = dirn[x]
            updated = res[x] - step * app[x]
            new_res[x] = updated
            new_dir[x] = updated * inv_diag[x] + correction[:, 128 * side : 128 * side + 128] + ratio * d
    for copy in sends:
        copy.wait_send()


def on_device(*args):
    block = jax.ShapeDtypeStruct((16, 16, 128), F32)
    return pl.pallas_call(
        kernel,
        out_shape=(block, block, block),
        in_specs=[pl.BlockSpec(memory_space=pltpu.HBM)] * 8,
        out_specs=(pl.BlockSpec(memory_space=pltpu.VMEM),) * 3,
        scratch_shapes=[
            pltpu.VMEM((16, 16, 128), F32),
            pltpu.VMEM((16, 16, 128), F32),
            pltpu.VMEM((16, 16, 128), F32),
            pltpu.SMEM((1,), F32),
            pltpu.VMEM((2, 16, 16), jnp.int32),
            pltpu.SMEM((1,), jnp.int32),
            pltpu.VMEM((64, 16, 16, 128), BF16),
            pltpu.VMEM((1024, 1024), F32),
            pltpu.VMEM((16, 128), F32),
            pltpu.VMEM((16, 128), F32),
            pltpu.VMEM((4, 16, 128), F32),
            pltpu.VMEM((16, 16, 128), F32),
            pltpu.VMEM((16, 16, 128), F32),
            pltpu.VMEM((32, 2048), BF16),
            pltpu.VMEM((32, 2048), BF16),
            pltpu.VMEM((1024, 128), BF16),
            pltpu.VMEM((8, 128), F32),
            pltpu.VMEM((8, 128), F32),
            pltpu.VMEM((16, 3, 128), F32),
            pltpu.VMEM((3, 256, 128), F32),
            pltpu.SemaphoreType.DMA((7,)),
            pltpu.SemaphoreType.DMA((8,)),
            pltpu.SemaphoreType.DMA((4,)),
            pltpu.SemaphoreType.DMA((4,)),
            pltpu.SemaphoreType.DMA((15,)),
            pltpu.SemaphoreType.DMA((15,)),
            pltpu.SemaphoreType.DMA((15,)),
            pltpu.SemaphoreType.DMA((15,)),
        ],
        compiler_params=pltpu.CompilerParams(
            collective_id=0, has_side_effects=True, vmem_limit_bytes=62 * 1024 * 1024
        ),
    )(*args)


def solution(mesh):
    field = P("stream", "span", None)
    in_specs = (
        field,
        field,
        field,
        P(),
        P(None, "stream", "span"),
        P(("stream", "span")),
        P(None, "stream", "span", None),
        P(),
    )
    return jax.shard_map(
        on_device, mesh=mesh, in_specs=in_specs, out_specs=(field, field, field), check_vma=False
    )
```

```python
import jax
import jax.numpy as jnp
from jax import lax
from jax.experimental import pallas as pl
from jax.experimental.pallas import tpu as pltpu
from jax.sharding import PartitionSpec as P

MESH = pl.DeviceIdType.MESH
F32 = jnp.float32
BF16 = jnp.bfloat16
NT = (((1,), (1,)), ((), ()))


def iota(shape, dim):
    return lax.broadcasted_iota(jnp.int32, shape, dim)


def split3(value):
    first = value.astype(BF16)
    rest = value - first.astype(F32)
    second = rest.astype(BF16)
    third = (rest - second.astype(F32)).astype(BF16)
    return first, second, third


def places():
    stream, z = lax.axis_index("stream"), lax.axis_index("span")
    y, x, core = stream // 8, lax.rem(stream // 2, 4), lax.rem(stream, 2)
    halo = [
        (lax.rem(stream + 1, 32), z),
        (lax.rem(stream + 31, 32), z),
        (stream, lax.rem(z + 1, 8)),
        (stream, lax.rem(z + 7, 8)),
    ]
    line = [
        ((y * 4 + x) * 2 + lax.rem(core + other, 2), lax.rem(z + away, 8))
        for away in (4, 3, 5, 2, 6, 1, 7, 0)
        for other in range(2)
        if away or other
    ]
    plane = [
        ((lax.rem(y + away // 4, 4) * 4 + lax.rem(x + away % 4, 4)) * 2 + core, z)
        for away in (10, 9, 11, 6, 14, 2, 8, 5, 7, 13, 15, 1, 3, 4, 12)
    ]
    return halo, line, plane, z * 2 + core, y * 4 + x, z


def kernel(
    res_hbm, dir_hbm, rz_hbm, wall_hbm, own_hbm, basis_hbm, inv_hbm,
    app, precond, step_row, ratio_row,
    res, dirn, rz, wall, own, basis, inv,
    low_face, high_face, halo_buf, inv_diag, w_res, w_app, group_sum, part_res, v_ref,
    line_buf, plane_buf,
    in_sem, basis_sem, halo_send, halo_recv, line_send, line_recv, plane_send, plane_recv,
):
    halo, line, plane, line_me, plane_me, z = places()
    barrier = pltpu.get_barrier_semaphore()
    for peer in halo + line + plane:
        pl.semaphore_signal(barrier, inc=1, device_id=peer, device_id_type=MESH)
    loads = [
        pltpu.make_async_copy(src, dst, in_sem.at[i])
        for i, (src, dst) in enumerate(
            ((dir_hbm, dirn), (wall_hbm, wall), (res_hbm, res), (rz_hbm, rz), (own_hbm, own), (inv_hbm, inv))
        )
    ]
    basis_loads = [
        pltpu.make_async_copy(basis_hbm.at[pl.ds(8 * i, 8)], basis.at[pl.ds(8 * i, 8)], basis_sem.at[i])
        for i in range(8)
    ]
    for load in loads[:5] + basis_loads + loads[5:]:
        load.start()

    lane = iota((16, 128), 1)
    row = iota((16, 128), 0)
    group_sum[...] = (iota((1024, 128), 0) // 16 == iota((1024, 128), 1) % 64).astype(F32).astype(BF16)

    loads[0].wait()
    for x in range(16):
        low_face[pl.ds(x, 1), :] = dirn[x, pl.ds(0, 1), :]
        high_face[pl.ds(x, 1), :] = dirn[x, pl.ds(15, 1), :]
    pl.semaphore_wait(barrier, len(halo + line + plane))
    sends = []
    for i, (src, peer) in enumerate(zip((dirn.at[15], dirn.at[0], high_face, low_face), halo)):
        copy = pltpu.make_async_remote_copy(
            src_ref=src, dst_ref=halo_buf.at[i], send_sem=halo_send.at[i], recv_sem=halo_recv.at[i],
            device_id=peer, device_id_type=MESH,
        )
        copy.start()
        sends.append(copy)

    loads[1].wait()
    loads[2].wait()
    same = iota((16, 16), 0) == iota((16, 16), 1)
    keep_low = (1 - wall[0]).astype(F32)
    keep_top = (1 - wall[1]).astype(F32)
    sum_rr = jnp.zeros((16, 128), F32)
    for x in range(16):
        own_d = dirn[x]
        low = jnp.sum(jnp.where(same, keep_low[x : x + 1, :], 0.0), axis=1, keepdims=True)
        top = jnp.sum(jnp.where(same, keep_top[x : x + 1, :], 0.0), axis=1, keepdims=True)
        around = jnp.where(lane == 0, own_d * low, pltpu.roll(own_d, 1, 1))
        around += jnp.where(lane == 127, own_d * top, pltpu.roll(own_d, 127, 1))
        around += jnp.where(row == 0, 0.0, pltpu.roll(own_d, 1, 0))
        around += jnp.where(row == 15, 0.0, pltpu.roll(own_d, 15, 0))
        if x > 0:
            around += dirn[x - 1]
        if x < 15:
            around += dirn[x + 1]
        app[x] = 6.0 * own_d - around
        diag = 6.0 - jnp.where(lane == 0, low, 0.0) - jnp.where(lane == 127, top, 0.0)
        inverse = 1.0 / diag
        inv_diag[x] = inverse
        r = res[x]
        sum_rr += r * r * inverse
        r_low = r.astype(BF16)
        w_res[0:16, 128 * x : 128 * x + 128] = r_low
        w_res[16:32, 128 * x : 128 * x + 128] = (r - r_low.astype(F32)).astype(BF16)

    pick = iota((32, 1024), 0) % 16 == iota((32, 1024), 1) % 16

    def slab(pair):
        return jnp.concatenate(
            [basis[:, 2 * pair].reshape(1024, 128), basis[:, 2 * pair + 1].reshape(1024, 128)], axis=1
        )

    def project(weights):
        total = jnp.zeros((32, 1024), F32)
        for pair in range(8):
            total += lax.dot_general(
                weights[:, 256 * pair : 256 * pair + 256], slab(pair), NT, preferred_element_type=F32
            )
        total = jnp.where(pick, total, 0.0)
        first = jnp.sum(total[0:16], axis=0, keepdims=True)
        second = jnp.sum(total[16:32], axis=0, keepdims=True)
        at = iota((8, 1024), 0)
        both = jnp.where(at == 0, first, jnp.where(at == 1, second, 0.0))
        one, two, three = (part.astype(F32) for part in split3(both))
        stacked = jnp.concatenate([one, two, three, jnp.zeros_like(one)], axis=0).astype(BF16)
        sums = jnp.dot(stacked, group_sum[...], preferred_element_type=F32)
        return sums[0:8] + sums[8:16] + sums[16:24]

    for load in basis_loads:
        load.wait()
    part_res[...] = project(w_res)

    for copy in sends:
        copy.wait_recv()
    from_low = jnp.where(z > 0, 1.0, 0.0)
    from_high = jnp.where(z < 7, 1.0, 0.0)
    sum_dq = jnp.zeros((16, 128), F32)
    sum_rq = jnp.zeros((16, 128), F32)
    sum_qq = jnp.zeros((16, 128), F32)
    for x in range(16):
        q = app[x]
        if x == 0:
            q -= halo_buf[0]
        if x == 15:
            q -= halo_buf[1]
        q -= jnp.where(row == 0, halo_buf[2, pl.ds(x, 1), :] * from_low, 0.0)
        q -= jnp.where(row == 15, halo_buf[3, pl.ds(x, 1), :] * from_high, 0.0)
        app[x] = q
        scaled = q * inv_diag[x]
        sum_dq += dirn[x] * q
        sum_rq += res[x] * scaled
        sum_qq += q * scaled
        q_low = q.astype(BF16)
        w_app[0:16, 128 * x : 128 * x + 128] = q_low
        w_app[16:32, 128 * x : 128 * x + 128] = (q - q_low.astype(F32)).astype(BF16)
    part_app = project(w_app)
    loads[4].wait()
    lane1 = lane[0:1]
    scalars = own[0, 0].astype(F32) * jnp.where(lane1 == 16 + line_me, 1.0, 0.0)
    for i, value in enumerate((sum_dq, sum_rr, sum_rq, sum_qq)):
        whole = jnp.sum(jnp.sum(value, axis=0, keepdims=True), axis=1, keepdims=True)
        scalars = jnp.where(lane1 == i, whole, scalars)
    line_buf[line_me, pl.ds(0, 1), :] = jnp.where(lane1 < 64, part_res[0:1, :], part_app[0:1, :])
    line_buf[line_me, pl.ds(1, 1), :] = jnp.where(lane1 < 64, part_res[1:2, :], part_app[1:2, :])
    line_buf[line_me, pl.ds(2, 1), :] = scalars

    copies = []
    for i, peer in enumerate(line):
        copy = pltpu.make_async_remote_copy(
            src_ref=line_buf.at[line_me], dst_ref=line_buf.at[line_me], send_sem=line_send.at[i],
            recv_sem=line_recv.at[i], device_id=peer, device_id_type=MESH,
        )
        copy.start()
        copies.append(copy)
    sends += copies
    for copy in copies:
        copy.wait_recv()
    for kind in range(2):
        plane_buf[plane_me, pl.ds(16 * kind, 16), :] = line_buf[:, kind, :]
    plane_buf[plane_me, pl.ds(32, 1), :] = jnp.sum(line_buf[:, 2, :], axis=0, keepdims=True)
    copies = []
    for i, peer in enumerate(plane):
        copy = pltpu.make_async_remote_copy(
            src_ref=plane_buf.at[plane_me], dst_ref=plane_buf.at[plane_me], send_sem=plane_send.at[i],
            recv_sem=plane_recv.at[i], device_id=peer, device_id_type=MESH,
        )
        copy.start()
        copies.append(copy)
    sends += copies
    loads[3].wait()
    loads[5].wait()
    for copy in copies:
        copy.wait_recv()

    scalars = plane_buf[:, 32, :]
    totals = jnp.sum(scalars, axis=0, keepdims=True)
    rz_old = rz[0, 0]
    step = rz_old / totals[:, 0:1]
    step_row[0] = jnp.broadcast_to(step, (1, 128))
    to_lanes = (iota((128, 256), 0) == 16 + iota((128, 256), 1) % 16).astype(F32).astype(BF16)
    owners = jnp.dot(jnp.where((lane >= 16) & (lane < 32), scalars, 0.0).astype(BF16), to_lanes, preferred_element_type=F32)
    owners = jnp.where(iota((16, 256), 0) == iota((16, 256), 1) // 16, owners, 0.0)
    owners = jnp.sum(owners, axis=0, keepdims=True)
    at = iota((16, 256), 0)
    wanted = jnp.where(at < 8, 2 * at, 2 * at - 15).astype(F32)
    chosen = (owners == wanted).astype(F32).astype(BF16)
    sums = jnp.zeros((16, 256), F32)
    for part in split3(jnp.concatenate([plane_buf[:, 0:16].reshape(256, 128), plane_buf[:, 16:32].reshape(256, 128)], axis=1)):
        sums += jnp.dot(chosen, part, preferred_element_type=F32)
    lane8 = iota((8, 128), 1)
    row8 = iota((8, 128), 0)

    def coarse(even, odd):
        return jnp.where(
            lane8 < 64, even - step * pltpu.roll(even, 64, 1), pltpu.roll(odd, 64, 1) - step * odd
        )

    rhs = coarse(sums[0:8, 0:128], sums[8:16, 0:128])
    rhs_rest = coarse(sums[0:8, 128:256], sums[8:16, 128:256])
    v_ref[...] = rhs

    def block(tile, total):
        values = v_ref[pl.ds(tile, 1), :]
        for k in range(16):
            column = jnp.sum(jnp.where(lane8 == row8 + 8 * k, values, 0.0), axis=1, keepdims=True)
            total += column * inv[pl.ds(pl.multiple_of(tile * 128 + 8 * k, 8), 8), :]
        return total

    total = lax.fori_loop(0, 8, block, jnp.zeros((8, 1024), F32))
    answer = jnp.zeros((8, 128), F32)
    for tile in range(8):
        answer = jnp.where(
            row8 == tile, jnp.sum(total[:, 128 * tile : 128 * tile + 128], axis=0, keepdims=True), answer
        )
    answer = answer.astype(BF16).astype(F32)
    inner = jnp.sum(jnp.sum(answer * (rhs + rhs_rest), axis=0, keepdims=True), axis=1, keepdims=True)
    rz_new = totals[:, 1:2] - 2.0 * step * totals[:, 2:3] + step * step * totals[:, 3:4] + inner
    ratio = rz_new / rz_old
    ratio_row[0] = jnp.broadcast_to(ratio, (1, 128))
    mine = own[0, 0]
    here = jnp.where(row8 == (mine >> 1), jnp.where((lane8 >> 6) == (mine & 1), answer, 0.0), 0.0)
    here = jnp.broadcast_to(jnp.sum(here, axis=0, keepdims=True), (16, 128)).astype(BF16)
    spread = lax.dot_general(here, group_sum[...], NT, preferred_element_type=F32)
    spread = jnp.where(pick[0:16], spread, 0.0).astype(BF16)
    for pair in range(8):
        correction = jnp.dot(spread, slab(pair), preferred_element_type=F32)
        for side in range(2):
            x = 2 * pair + side
            updated = res[x] - step * app[x]
            precond[x] = updated * inv_diag[x] + correction[:, 128 * side : 128 * side + 128]
    for copy in sends:
        copy.wait_send()


def on_device(solution, residual, direction, rz_old, wall_flags, owner_list, coarse_basis, coarse_inverse):
    block = pltpu.VMEM((16, 16, 128), F32)
    line = pltpu.VMEM((1, 1, 128), F32)
    applied, precond, step, ratio = pl.pallas_call(
        kernel,
        out_shape=(block, block, line, line),
        in_specs=[pl.BlockSpec(memory_space=pltpu.HBM)] * 7,
        out_specs=(pl.BlockSpec(memory_space=pltpu.VMEM),) * 4,
        scratch_shapes=[
            pltpu.VMEM((16, 16, 128), F32),
            pltpu.VMEM((16, 16, 128), F32),
            pltpu.SMEM((1, 1), F32),
            pltpu.VMEM((2, 16, 16), jnp.int32),
            pltpu.SMEM((1, 1), jnp.int32),
            pltpu.VMEM((64, 16, 16, 128), BF16),
            pltpu.VMEM((1024, 1024), F32),
            pltpu.VMEM((16, 128), F32),
            pltpu.VMEM((16, 128), F32),
            pltpu.VMEM((4, 16, 128), F32),
            pltpu.VMEM((16, 16, 128), F32),
            pltpu.VMEM((32, 2048), BF16),
            pltpu.VMEM((32, 2048), BF16),
            pltpu.VMEM((1024, 128), BF16),
            pltpu.VMEM((8, 128), F32),
            pltpu.VMEM((8, 128), F32),
            pltpu.VMEM((16, 3, 128), F32),
            pltpu.VMEM((16, 33, 128), F32),
            pltpu.SemaphoreType.DMA((6,)),
            pltpu.SemaphoreType.DMA((8,)),
            pltpu.SemaphoreType.DMA((4,)),
            pltpu.SemaphoreType.DMA((4,)),
            pltpu.SemaphoreType.DMA((15,)),
            pltpu.SemaphoreType.DMA((15,)),
            pltpu.SemaphoreType.DMA((15,)),
            pltpu.SemaphoreType.DMA((15,)),
        ],
        compiler_params=pltpu.CompilerParams(
            collective_id=0, has_side_effects=True, vmem_limit_bytes=62 * 1024 * 1024
        ),
    )(residual, direction, rz_old.reshape(1, 1), wall_flags, owner_list.reshape(1, 1), coarse_basis, coarse_inverse)
    return solution + step * direction, residual - step * applied, precond + ratio * direction


def solution(mesh):
    field = P("stream", "span", None)
    in_specs = (
        field,
        field,
        field,
        P(),
        P(None, "stream", "span"),
        P(("stream", "span")),
        P(None, "stream", "span", None),
        P(),
    )
    return jax.shard_map(
        on_device, mesh=mesh, in_specs=in_specs, out_specs=(field, field, field), check_vma=False
    )
```

```python
import jax
import jax.numpy as jnp
from jax import lax
from jax.experimental import pallas as pl
from jax.experimental.pallas import tpu as pltpu
from jax.sharding import PartitionSpec as P

MESH = pl.DeviceIdType.MESH
F32 = jnp.float32
BF16 = jnp.bfloat16
NT = (((1,), (1,)), ((), ()))


def iota(shape, dim):
    return lax.broadcasted_iota(jnp.int32, shape, dim)


def split3(value):
    first = value.astype(BF16)
    rest = value - first.astype(F32)
    second = rest.astype(BF16)
    third = (rest - second.astype(F32)).astype(BF16)
    return first, second, third


def places():
    stream, z = lax.axis_index("stream"), lax.axis_index("span")
    y, x, core = stream // 8, lax.rem(stream // 2, 4), lax.rem(stream, 2)
    halo = [
        (lax.rem(stream + 1, 32), z),
        (lax.rem(stream + 31, 32), z),
        (stream, lax.rem(z + 1, 8)),
        (stream, lax.rem(z + 7, 8)),
    ]
    line = [
        ((y * 4 + x) * 2 + lax.rem(core + other, 2), lax.rem(z + away, 8))
        for away in (4, 3, 5, 2, 6, 1, 7, 0)
        for other in range(2)
        if away or other
    ]
    plane = [
        ((lax.rem(y + away // 4, 4) * 4 + lax.rem(x + away % 4, 4)) * 2 + core, z)
        for away in (10, 9, 11, 6, 14, 2, 8, 5, 7, 13, 15, 1, 3, 4, 12)
    ]
    return halo, line, plane, z * 2 + core, y * 4 + x, z


def kernel(
    res_hbm, dir_hbm, rz_hbm, wall_hbm, own_hbm, basis_hbm, inv_hbm,
    app, precond, step_row, ratio_row,
    res, dirn, rz, wall, own, basis, inv,
    low_face, high_face, halo_buf, inv_diag, w_res, w_app, group_sum, per_cell, part_res, v_ref,
    line_buf, plane_buf,
    in_sem, basis_sem, halo_send, halo_recv, line_send, line_recv, plane_send, plane_recv,
):
    halo, line, plane, line_me, plane_me, z = places()
    barrier = pltpu.get_barrier_semaphore()
    for peer in line[:2] + plane[:1] + line[2:6] + plane[1:5] + halo[:2] + line[6:10] + plane[5:] + line[10:] + halo[2:]:
        pl.semaphore_signal(barrier, inc=1, device_id=peer, device_id_type=MESH)
    loads = [
        pltpu.make_async_copy(src, dst, in_sem.at[i])
        for i, (src, dst) in enumerate(
            ((dir_hbm, dirn), (wall_hbm, wall), (res_hbm, res), (rz_hbm, rz), (own_hbm, own), (inv_hbm, inv))
        )
    ]
    basis_loads = [
        pltpu.make_async_copy(basis_hbm.at[pl.ds(8 * i, 8)], basis.at[pl.ds(8 * i, 8)], basis_sem.at[i])
        for i in range(8)
    ]
    for load in loads[:5] + basis_loads + loads[5:]:
        load.start()

    lane = iota((16, 128), 1)
    row = iota((16, 128), 0)
    group_sum[...] = (iota((1024, 128), 0) // 16 == iota((1024, 128), 1) % 64).astype(F32).astype(BF16)
    per_cell[...] = (iota((128, 1024), 0) % 64 == iota((128, 1024), 1) // 16).astype(F32).astype(BF16)

    loads[0].wait()
    for x in range(16):
        low_face[pl.ds(x, 1), :] = dirn[x, pl.ds(0, 1), :]
        high_face[pl.ds(x, 1), :] = dirn[x, pl.ds(15, 1), :]
    pl.semaphore_wait(barrier, len(halo + line + plane))
    sends = []
    for i, (src, peer) in enumerate(zip((dirn.at[15], dirn.at[0], high_face, low_face), halo)):
        copy = pltpu.make_async_remote_copy(
            src_ref=src, dst_ref=halo_buf.at[i], send_sem=halo_send.at[i], recv_sem=halo_recv.at[i],
            device_id=peer, device_id_type=MESH,
        )
        copy.start()
        sends.append(copy)

    loads[1].wait()
    loads[2].wait()
    same = iota((16, 16), 0) == iota((16, 16), 1)
    keep_low = (1 - wall[0]).astype(F32)
    keep_top = (1 - wall[1]).astype(F32)
    sum_rr = jnp.zeros((16, 128), F32)
    for x in range(16):
        own_d = dirn[x]
        low = jnp.sum(jnp.where(same, keep_low[x : x + 1, :], 0.0), axis=1, keepdims=True)
        top = jnp.sum(jnp.where(same, keep_top[x : x + 1, :], 0.0), axis=1, keepdims=True)
        around = jnp.where(lane == 0, own_d * low, pltpu.roll(own_d, 1, 1))
        around += jnp.where(lane == 127, own_d * top, pltpu.roll(own_d, 127, 1))
        around += jnp.where(row == 0, 0.0, pltpu.roll(own_d, 1, 0))
        around += jnp.where(row == 15, 0.0, pltpu.roll(own_d, 15, 0))
        if x > 0:
            around += dirn[x - 1]
        if x < 15:
            around += dirn[x + 1]
        app[x] = 6.0 * own_d - around
        diag = 6.0 - jnp.where(lane == 0, low, 0.0) - jnp.where(lane == 127, top, 0.0)
        inverse = 1.0 / diag
        inv_diag[x] = inverse
        r = res[x]
        sum_rr += r * r * inverse
        r_low = r.astype(BF16)
        w_res[0:16, 128 * x : 128 * x + 128] = r_low
        w_res[16:32, 128 * x : 128 * x + 128] = (r - r_low.astype(F32)).astype(BF16)

    pick = iota((32, 1024), 0) % 16 == iota((32, 1024), 1) % 16

    def slab(pair):
        return jnp.concatenate(
            [basis[:, 2 * pair].reshape(1024, 128), basis[:, 2 * pair + 1].reshape(1024, 128)], axis=1
        )

    def project(weights):
        total = jnp.zeros((32, 1024), F32)
        for pair in range(8):
            total += lax.dot_general(
                weights[:, 256 * pair : 256 * pair + 256], slab(pair), NT, preferred_element_type=F32
            )
        total = jnp.where(pick, total, 0.0)
        first = jnp.sum(total[0:16], axis=0, keepdims=True)
        second = jnp.sum(total[16:32], axis=0, keepdims=True)
        at = iota((8, 1024), 0)
        both = jnp.where(at == 0, first, jnp.where(at == 1, second, 0.0))
        one, two, three = (part.astype(F32) for part in split3(both))
        stacked = jnp.concatenate([one, two, three, jnp.zeros_like(one)], axis=0).astype(BF16)
        sums = jnp.dot(stacked, group_sum[...], preferred_element_type=F32)
        return sums[0:8] + sums[8:16] + sums[16:24]

    for load in basis_loads:
        load.wait()
    part_res[...] = project(w_res)

    for copy in sends:
        copy.wait_recv()
    from_low = jnp.where(z > 0, 1.0, 0.0)
    from_high = jnp.where(z < 7, 1.0, 0.0)
    sum_dq = jnp.zeros((16, 128), F32)
    sum_rq = jnp.zeros((16, 128), F32)
    sum_qq = jnp.zeros((16, 128), F32)
    for x in range(16):
        q = app[x]
        if x == 0:
            q -= halo_buf[0]
        if x == 15:
            q -= halo_buf[1]
        q -= jnp.where(row == 0, halo_buf[2, pl.ds(x, 1), :] * from_low, 0.0)
        q -= jnp.where(row == 15, halo_buf[3, pl.ds(x, 1), :] * from_high, 0.0)
        app[x] = q
        scaled = q * inv_diag[x]
        sum_dq += dirn[x] * q
        sum_rq += res[x] * scaled
        sum_qq += q * scaled
        q_low = q.astype(BF16)
        w_app[0:16, 128 * x : 128 * x + 128] = q_low
        w_app[16:32, 128 * x : 128 * x + 128] = (q - q_low.astype(F32)).astype(BF16)
    part_app = project(w_app)
    loads[4].wait()
    lane1 = lane[0:1]
    scalars = own[0, 0].astype(F32) * jnp.where(lane1 == 16 + line_me, 1.0, 0.0)
    for i, value in enumerate((sum_dq, sum_rr, sum_rq, sum_qq)):
        whole = jnp.sum(jnp.sum(value, axis=0, keepdims=True), axis=1, keepdims=True)
        scalars = jnp.where(lane1 == i, whole, scalars)
    line_buf[line_me, pl.ds(0, 1), :] = jnp.where(lane1 < 64, part_res[0:1, :], part_app[0:1, :])
    line_buf[line_me, pl.ds(1, 1), :] = jnp.where(lane1 < 64, part_res[1:2, :], part_app[1:2, :])
    line_buf[line_me, pl.ds(2, 1), :] = scalars

    copies = []
    for i, peer in enumerate(line):
        copy = pltpu.make_async_remote_copy(
            src_ref=line_buf.at[line_me], dst_ref=line_buf.at[line_me], send_sem=line_send.at[i],
            recv_sem=line_recv.at[i], device_id=peer, device_id_type=MESH,
        )
        copy.start()
        copies.append(copy)
    sends += copies
    for copy in copies:
        copy.wait_recv()
    for kind in range(2):
        plane_buf[plane_me, pl.ds(16 * kind, 16), :] = line_buf[:, kind, :]
    plane_buf[plane_me, pl.ds(32, 1), :] = jnp.sum(line_buf[:, 2, :], axis=0, keepdims=True)
    copies = []
    for i, peer in enumerate(plane):
        copy = pltpu.make_async_remote_copy(
            src_ref=plane_buf.at[plane_me], dst_ref=plane_buf.at[plane_me], send_sem=plane_send.at[i],
            recv_sem=plane_recv.at[i], device_id=peer, device_id_type=MESH,
        )
        copy.start()
        copies.append(copy)
    sends += copies
    loads[3].wait()
    loads[5].wait()
    for copy in copies:
        copy.wait_recv()

    scalars = plane_buf[:, 32, :]
    totals = jnp.sum(scalars, axis=0, keepdims=True)
    rz_old = rz[0, 0]
    step = rz_old / totals[:, 0:1]
    step_row[0] = jnp.broadcast_to(step, (1, 128))
    to_lanes = (iota((128, 256), 0) == 16 + iota((128, 256), 1) % 16).astype(F32).astype(BF16)
    owners = jnp.dot(jnp.where((lane >= 16) & (lane < 32), scalars, 0.0).astype(BF16), to_lanes, preferred_element_type=F32)
    owners = jnp.where(iota((16, 256), 0) == iota((16, 256), 1) // 16, owners, 0.0)
    owners = jnp.sum(owners, axis=0, keepdims=True)
    at = iota((16, 256), 0)
    wanted = jnp.where(at < 8, 2 * at, 2 * at - 15).astype(F32)
    chosen = (owners == wanted).astype(F32).astype(BF16)
    sums = jnp.zeros((16, 256), F32)
    for part in split3(jnp.concatenate([plane_buf[:, 0:16].reshape(256, 128), plane_buf[:, 16:32].reshape(256, 128)], axis=1)):
        sums += jnp.dot(chosen, part, preferred_element_type=F32)
    lane8 = iota((8, 128), 1)
    row8 = iota((8, 128), 0)

    def coarse(even, odd):
        return jnp.where(
            lane8 < 64, even - step * pltpu.roll(even, 64, 1), pltpu.roll(odd, 64, 1) - step * odd
        )

    rhs = coarse(sums[0:8, 0:128], sums[8:16, 0:128])
    rhs_rest = coarse(sums[0:8, 128:256], sums[8:16, 128:256])
    v_ref[...] = rhs

    def block(tile, total):
        values = v_ref[pl.ds(tile, 1), :]
        for k in range(16):
            column = jnp.sum(jnp.where(lane8 == row8 + 8 * k, values, 0.0), axis=1, keepdims=True)
            total += column * inv[pl.ds(pl.multiple_of(tile * 128 + 8 * k, 8), 8), :]
        return total

    total = lax.fori_loop(0, 8, block, jnp.zeros((8, 1024), F32), unroll=True)
    answer = jnp.zeros((8, 128), F32)
    for tile in range(8):
        answer = jnp.where(
            row8 == tile, jnp.sum(total[:, 128 * tile : 128 * tile + 128], axis=0, keepdims=True), answer
        )
    answer = answer.astype(BF16).astype(F32)
    inner = jnp.sum(jnp.sum(answer * (rhs + rhs_rest), axis=0, keepdims=True), axis=1, keepdims=True)
    rz_new = totals[:, 1:2] - 2.0 * step * totals[:, 2:3] + step * step * totals[:, 3:4] + inner
    ratio = rz_new / rz_old
    ratio_row[0] = jnp.broadcast_to(ratio, (1, 128))
    mine = own[0, 0]
    here = jnp.where(row8 == (mine >> 1), jnp.where((lane8 >> 6) == (mine & 1), answer, 0.0), 0.0)
    here = jnp.broadcast_to(jnp.sum(here, axis=0, keepdims=True), (16, 128)).astype(BF16)
    spread = jnp.dot(here, per_cell[...], preferred_element_type=F32)
    spread = jnp.where(pick[0:16], spread, 0.0).astype(BF16)
    for pair in range(8):
        correction = jnp.dot(spread, slab(pair), preferred_element_type=F32)
        for side in range(2):
            x = 2 * pair + side
            updated = res[x] - step * app[x]
            precond[x] = updated * inv_diag[x] + correction[:, 128 * side : 128 * side + 128]
    for copy in sends:
        copy.wait_send()


def on_device(solution, residual, direction, rz_old, wall_flags, owner_list, coarse_basis, coarse_inverse):
    block = pltpu.VMEM((16, 16, 128), F32)
    line = pltpu.VMEM((1, 1, 128), F32)
    applied, precond, step, ratio = pl.pallas_call(
        kernel,
        out_shape=(block, block, line, line),
        in_specs=[pl.BlockSpec(memory_space=pltpu.HBM)] * 7,
        out_specs=(pl.BlockSpec(memory_space=pltpu.VMEM),) * 4,
        scratch_shapes=[
            pltpu.VMEM((16, 16, 128), F32),
            pltpu.VMEM((16, 16, 128), F32),
            pltpu.SMEM((1, 1), F32),
            pltpu.VMEM((2, 16, 16), jnp.int32),
            pltpu.SMEM((1, 1), jnp.int32),
            pltpu.VMEM((64, 16, 16, 128), BF16),
            pltpu.VMEM((1024, 1024), F32),
            pltpu.VMEM((16, 128), F32),
            pltpu.VMEM((16, 128), F32),
            pltpu.VMEM((4, 16, 128), F32),
            pltpu.VMEM((16, 16, 128), F32),
            pltpu.VMEM((32, 2048), BF16),
            pltpu.VMEM((32, 2048), BF16),
            pltpu.VMEM((1024, 128), BF16),
            pltpu.VMEM((128, 1024), BF16),
            pltpu.VMEM((8, 128), F32),
            pltpu.VMEM((8, 128), F32),
            pltpu.VMEM((16, 3, 128), F32),
            pltpu.VMEM((16, 33, 128), F32),
            pltpu.SemaphoreType.DMA((6,)),
            pltpu.SemaphoreType.DMA((8,)),
            pltpu.SemaphoreType.DMA((4,)),
            pltpu.SemaphoreType.DMA((4,)),
            pltpu.SemaphoreType.DMA((15,)),
            pltpu.SemaphoreType.DMA((15,)),
            pltpu.SemaphoreType.DMA((15,)),
            pltpu.SemaphoreType.DMA((15,)),
        ],
        compiler_params=pltpu.CompilerParams(
            collective_id=0, has_side_effects=True, vmem_limit_bytes=62 * 1024 * 1024
        ),
    )(residual, direction, rz_old.reshape(1, 1), wall_flags, owner_list.reshape(1, 1), coarse_basis, coarse_inverse)
    return solution + step * direction, residual - step * applied, precond + ratio * direction


def solution(mesh):
    field = P("stream", "span", None)
    in_specs = (
        field,
        field,
        field,
        P(),
        P(None, "stream", "span"),
        P(("stream", "span")),
        P(None, "stream", "span", None),
        P(),
    )
    return jax.shard_map(
        on_device, mesh=mesh, in_specs=in_specs, out_specs=(field, field, field), check_vma=False
    )
```

```python
import jax
import jax.numpy as jnp
from jax import lax
from jax.experimental import pallas as pl
from jax.experimental.pallas import tpu as pltpu
from jax.sharding import PartitionSpec as P

MESH = pl.DeviceIdType.MESH
F32 = jnp.float32
BF16 = jnp.bfloat16
NT = (((1,), (1,)), ((), ()))


def iota(shape, dim):
    return lax.broadcasted_iota(jnp.int32, shape, dim)


def split3(value):
    first = value.astype(BF16)
    rest = value - first.astype(F32)
    second = rest.astype(BF16)
    third = (rest - second.astype(F32)).astype(BF16)
    return first, second, third


def places():
    stream, z = lax.axis_index("stream"), lax.axis_index("span")
    y, x, core = stream // 8, lax.rem(stream // 2, 4), lax.rem(stream, 2)
    halo = [
        (lax.rem(stream + 1, 32), z),
        (lax.rem(stream + 31, 32), z),
        (stream, lax.rem(z + 1, 8)),
        (stream, lax.rem(z + 7, 8)),
    ]
    line = [
        ((y * 4 + x) * 2 + lax.rem(core + other, 2), lax.rem(z + away, 8))
        for away in (4, 3, 5, 2, 6, 1, 7, 0)
        for other in range(2)
        if away or other
    ]
    plane = [
        ((lax.rem(y + away // 4, 4) * 4 + lax.rem(x + away % 4, 4)) * 2 + core, z)
        for away in (10, 9, 11, 6, 14, 2, 8, 5, 7, 13, 15, 1, 3, 4, 12)
    ]
    return halo, line, plane, z * 2 + core, y * 4 + x, z


def kernel(
    res_hbm, dir_hbm, rz_hbm, wall_hbm, own_hbm, basis_hbm, inv_hbm,
    app, precond, step_row, ratio_row,
    res, dirn, rz, wall, own, basis, inv,
    low_face, high_face, halo_buf, inv_diag, w_all, w_faces, w_rows, edge, group_sum, per_cell, early, v_ref,
    line_buf, plane_buf,
    in_sem, basis_sem, halo_send, halo_recv, line_send, line_recv, plane_send, plane_recv,
):
    halo, line, plane, line_me, plane_me, z = places()
    loads = [
        pltpu.make_async_copy(src, dst, in_sem.at[i])
        for i, (src, dst) in enumerate(
            ((dir_hbm, dirn), (wall_hbm, wall), (res_hbm, res), (rz_hbm, rz), (own_hbm, own), (inv_hbm, inv))
        )
    ]
    loads[0].start()
    barrier = pltpu.get_barrier_semaphore()
    for peer in line[:2] + plane[:1] + line[2:6] + plane[1:5] + halo[:2] + line[6:10] + plane[5:] + line[10:] + halo[2:]:
        pl.semaphore_signal(barrier, inc=1, device_id=peer, device_id_type=MESH)
    basis_loads = [
        pltpu.make_async_copy(basis_hbm.at[pl.ds(8 * i, 8)], basis.at[pl.ds(8 * i, 8)], basis_sem.at[i])
        for i in range(8)
    ]
    for load in loads[1:5] + basis_loads + loads[5:]:
        load.start()

    lane = iota((16, 128), 1)
    row = iota((16, 128), 0)
    group_sum[0:1024, :] = (iota((1024, 128), 0) // 16 == iota((1024, 128), 1) % 64).astype(F32).astype(BF16)
    group_sum[1024:1152, :] = (iota((128, 128), 0) // 2 == iota((128, 128), 1) % 64).astype(F32).astype(BF16)
    per_cell[...] = (iota((128, 1024), 0) % 64 == iota((128, 1024), 1) // 16).astype(F32).astype(BF16)

    loads[0].wait()
    for x in range(16):
        low_face[pl.ds(x, 1), :] = dirn[x, pl.ds(0, 1), :]
        high_face[pl.ds(x, 1), :] = dirn[x, pl.ds(15, 1), :]
    pl.semaphore_wait(barrier, len(halo + line + plane))
    sends = []
    for i, (src, peer) in enumerate(zip((dirn.at[15], dirn.at[0], high_face, low_face), halo)):
        copy = pltpu.make_async_remote_copy(
            src_ref=src, dst_ref=halo_buf.at[i], send_sem=halo_send.at[i], recv_sem=halo_recv.at[i],
            device_id=peer, device_id_type=MESH,
        )
        copy.start()
        sends.append(copy)

    loads[1].wait()
    loads[2].wait()
    same = iota((16, 16), 0) == iota((16, 16), 1)
    keep_low = (1 - wall[0]).astype(F32)
    keep_top = (1 - wall[1]).astype(F32)
    sum_rr = jnp.zeros((16, 128), F32)
    for x in range(16):
        own_d = dirn[x]
        low = jnp.sum(jnp.where(same, keep_low[x : x + 1, :], 0.0), axis=1, keepdims=True)
        top = jnp.sum(jnp.where(same, keep_top[x : x + 1, :], 0.0), axis=1, keepdims=True)
        around = jnp.where(lane == 0, own_d * low, pltpu.roll(own_d, 1, 1))
        around += jnp.where(lane == 127, own_d * top, pltpu.roll(own_d, 127, 1))
        around += jnp.where(row == 0, 0.0, pltpu.roll(own_d, 1, 0))
        around += jnp.where(row == 15, 0.0, pltpu.roll(own_d, 15, 0))
        if x > 0:
            around += dirn[x - 1]
        if x < 15:
            around += dirn[x + 1]
        app[x] = 6.0 * own_d - around
        diag = 6.0 - jnp.where(lane == 0, low, 0.0) - jnp.where(lane == 127, top, 0.0)
        inverse = 1.0 / diag
        inv_diag[x] = inverse
        r = res[x]
        sum_rr += r * r * inverse
        r_low = r.astype(BF16)
        at = slice(128 * x, 128 * x + 128)
        w_all[0:16, at] = r_low
        w_all[16:32, at] = (r - r_low.astype(F32)).astype(BF16)
        if 0 < x < 15:
            inner = jnp.where((row > 0) & (row < 15), app[x], 0.0)
        else:
            inner = jnp.zeros((16, 128), F32)
            w_rows[:, at] = inner.astype(BF16)
        q_low = inner.astype(BF16)
        w_all[32:48, at] = q_low
        w_all[48:64, at] = (inner - q_low.astype(F32)).astype(BF16)

    pick = iota((64, 1024), 0) % 16 == iota((64, 1024), 1) % 16

    def slab(low, high):
        return jnp.concatenate([basis[:, low].reshape(1024, 128), basis[:, high].reshape(1024, 128)], axis=1)

    def picked(total):
        total = jnp.where(pick[0 : total.shape[0]], total, 0.0)
        return [jnp.sum(total[16 * i : 16 * i + 16], axis=0, keepdims=True) for i in range(total.shape[0] // 16)]

    def stack(lines):
        at = iota((8, lines[0].shape[1]), 0)
        total = jnp.zeros(at.shape, F32)
        for i, line in enumerate(lines):
            total = jnp.where(at == i, line, total)
        return total

    def by_basis(both, groups):
        one, two, three = (part.astype(F32) for part in split3(both))
        stacked = jnp.concatenate([one, two, three, jnp.zeros_like(one)], axis=0).astype(BF16)
        sums = jnp.dot(stacked, groups, preferred_element_type=F32)
        return sums[0:8] + sums[8:16] + sums[16:24]

    for load in basis_loads:
        load.wait()
    total = jnp.zeros((64, 1024), F32)
    for pair in range(8):
        total += lax.dot_general(
            w_all[:, 256 * pair : 256 * pair + 256], slab(2 * pair, 2 * pair + 1), NT, preferred_element_type=F32
        )
    early[...] = by_basis(stack(picked(total)), group_sum[0:1024, :])
    choose = (
        (iota((32, 256), 0) // 2 == iota((32, 256), 1) // 16)
        & (iota((32, 256), 1) % 16 == 15 * (iota((32, 256), 0) % 2))
    ).astype(F32).astype(BF16)
    for part in range(4):
        for pair in range(8):
            tile = jnp.concatenate(
                [basis[16 * part : 16 * part + 16, 2 * pair + i].reshape(256, 128) for i in range(2)], axis=1
            )
            edge[32 * part : 32 * part + 32, 256 * pair : 256 * pair + 256] = jnp.dot(
                choose, tile, preferred_element_type=F32
            ).astype(BF16)

    for copy in sends:
        copy.wait_recv()
    from_low = jnp.where(z > 0, 1.0, 0.0)
    from_high = jnp.where(z < 7, 1.0, 0.0)
    sum_dq = jnp.zeros((16, 128), F32)
    sum_rq = jnp.zeros((16, 128), F32)
    sum_qq = jnp.zeros((16, 128), F32)
    for x in range(16):
        q = app[x]
        if x == 0:
            q -= halo_buf[0]
        if x == 15:
            q -= halo_buf[1]
        q -= jnp.where(row == 0, halo_buf[2, pl.ds(x, 1), :] * from_low, 0.0)
        q -= jnp.where(row == 15, halo_buf[3, pl.ds(x, 1), :] * from_high, 0.0)
        app[x] = q
        scaled = q * inv_diag[x]
        sum_dq += dirn[x] * q
        sum_rq += res[x] * scaled
        sum_qq += q * scaled
        q_low = q.astype(BF16)
        q_rest = q - q_low.astype(F32)
        if x in (0, 15):
            at = slice(0, 128) if x == 0 else slice(128, 256)
            w_faces[0:16, at] = q_low
            w_faces[16:32, at] = q_rest.astype(BF16)
        else:
            q_low = q_low.astype(F32)
            ends = jnp.where(row == 0, q_low[0:1], jnp.where(row == 1, q_low[15:16], 0.0))
            ends = jnp.where(row == 2, q_rest[0:1], jnp.where(row == 3, q_rest[15:16], ends))
            w_rows[:, 128 * x : 128 * x + 128] = ends.astype(BF16)
    faces = picked(lax.dot_general(w_faces[...], slab(0, 15), NT, preferred_element_type=F32))
    ends = lax.dot_general(w_rows[...], edge[...], NT, preferred_element_type=F32)
    ends = jnp.where(row % 2 == lane % 2, ends, 0.0)
    late = by_basis(
        jnp.concatenate([stack(faces), stack([ends[0:1] + ends[1:2], ends[2:3] + ends[3:4]])], axis=1), group_sum[...]
    )
    part_res = early[...]
    part_app = part_res[2:4] + late[0:2]
    loads[4].wait()
    lane1 = lane[0:1]
    scalars = own[0, 0].astype(F32) * jnp.where(lane1 == 16 + line_me, 1.0, 0.0)
    for i, value in enumerate((sum_dq, sum_rr, sum_rq, sum_qq)):
        whole = jnp.sum(jnp.sum(value, axis=0, keepdims=True), axis=1, keepdims=True)
        scalars = jnp.where(lane1 == i, whole, scalars)
    line_buf[line_me, pl.ds(0, 1), :] = jnp.where(lane1 < 64, part_res[0:1, :], part_app[0:1, :])
    line_buf[line_me, pl.ds(1, 1), :] = jnp.where(lane1 < 64, part_res[1:2, :], part_app[1:2, :])
    line_buf[line_me, pl.ds(2, 1), :] = scalars

    copies = []
    for i, peer in enumerate(line):
        copy = pltpu.make_async_remote_copy(
            src_ref=line_buf.at[line_me], dst_ref=line_buf.at[line_me], send_sem=line_send.at[i],
            recv_sem=line_recv.at[i], device_id=peer, device_id_type=MESH,
        )
        copy.start()
        copies.append(copy)
    sends += copies
    for copy in copies:
        copy.wait_recv()
    for kind in range(2):
        plane_buf[plane_me, pl.ds(16 * kind, 16), :] = line_buf[:, kind, :]
    plane_buf[plane_me, pl.ds(32, 1), :] = jnp.sum(line_buf[:, 2, :], axis=0, keepdims=True)
    copies = []
    for i, peer in enumerate(plane):
        copy = pltpu.make_async_remote_copy(
            src_ref=plane_buf.at[plane_me], dst_ref=plane_buf.at[plane_me], send_sem=plane_send.at[i],
            recv_sem=plane_recv.at[i], device_id=peer, device_id_type=MESH,
        )
        copy.start()
        copies.append(copy)
    sends += copies
    loads[3].wait()
    loads[5].wait()
    for copy in copies:
        copy.wait_recv()

    scalars = plane_buf[:, 32, :]
    totals = jnp.sum(scalars, axis=0, keepdims=True)
    rz_old = rz[0, 0]
    step = rz_old / totals[:, 0:1]
    step_row[0] = jnp.broadcast_to(step, (1, 128))
    to_lanes = (iota((128, 256), 0) == 16 + iota((128, 256), 1) % 16).astype(F32).astype(BF16)
    owners = jnp.dot(jnp.where((lane >= 16) & (lane < 32), scalars, 0.0).astype(BF16), to_lanes, preferred_element_type=F32)
    owners = jnp.where(iota((16, 256), 0) == iota((16, 256), 1) // 16, owners, 0.0)
    owners = jnp.sum(owners, axis=0, keepdims=True)
    at = iota((16, 256), 0)
    wanted = jnp.where(at < 8, 2 * at, 2 * at - 15).astype(F32)
    chosen = (owners == wanted).astype(F32).astype(BF16)
    sums = jnp.zeros((16, 256), F32)
    for part in split3(jnp.concatenate([plane_buf[:, 0:16].reshape(256, 128), plane_buf[:, 16:32].reshape(256, 128)], axis=1)):
        sums += jnp.dot(chosen, part, preferred_element_type=F32)
    lane8 = iota((8, 128), 1)
    row8 = iota((8, 128), 0)

    def coarse(even, odd):
        return jnp.where(
            lane8 < 64, even - step * pltpu.roll(even, 64, 1), pltpu.roll(odd, 64, 1) - step * odd
        )

    rhs = coarse(sums[0:8, 0:128], sums[8:16, 0:128])
    rhs_rest = coarse(sums[0:8, 128:256], sums[8:16, 128:256])
    v_ref[...] = rhs

    def block(tile, total):
        values = v_ref[pl.ds(tile, 1), :]
        for k in range(16):
            column = jnp.sum(jnp.where(lane8 == row8 + 8 * k, values, 0.0), axis=1, keepdims=True)
            total += column * inv[pl.ds(pl.multiple_of(tile * 128 + 8 * k, 8), 8), :]
        return total

    total = lax.fori_loop(0, 8, block, jnp.zeros((8, 1024), F32), unroll=True)
    answer = jnp.zeros((8, 128), F32)
    for tile in range(8):
        answer = jnp.where(
            row8 == tile, jnp.sum(total[:, 128 * tile : 128 * tile + 128], axis=0, keepdims=True), answer
        )
    answer = answer.astype(BF16).astype(F32)
    inner = jnp.sum(jnp.sum(answer * (rhs + rhs_rest), axis=0, keepdims=True), axis=1, keepdims=True)
    rz_new = totals[:, 1:2] - 2.0 * step * totals[:, 2:3] + step * step * totals[:, 3:4] + inner
    ratio = rz_new / rz_old
    ratio_row[0] = jnp.broadcast_to(ratio, (1, 128))
    mine = own[0, 0]
    here = jnp.where(row8 == (mine >> 1), jnp.where((lane8 >> 6) == (mine & 1), answer, 0.0), 0.0)
    here = jnp.broadcast_to(jnp.sum(here, axis=0, keepdims=True), (16, 128)).astype(BF16)
    spread = jnp.dot(here, per_cell[...], preferred_element_type=F32)
    spread = jnp.where(pick[0:16], spread, 0.0).astype(BF16)
    for pair in range(8):
        correction = jnp.dot(spread, slab(2 * pair, 2 * pair + 1), preferred_element_type=F32)
        for side in range(2):
            x = 2 * pair + side
            updated = res[x] - step * app[x]
            precond[x] = updated * inv_diag[x] + correction[:, 128 * side : 128 * side + 128]
    for copy in sends:
        copy.wait_send()


def on_device(solution, residual, direction, rz_old, wall_flags, owner_list, coarse_basis, coarse_inverse):
    block = pltpu.VMEM((16, 16, 128), F32)
    line = pltpu.VMEM((1, 1, 128), F32)
    applied, precond, step, ratio = pl.pallas_call(
        kernel,
        out_shape=(block, block, line, line),
        in_specs=[pl.BlockSpec(memory_space=pltpu.HBM)] * 7,
        out_specs=(pl.BlockSpec(memory_space=pltpu.VMEM),) * 4,
        scratch_shapes=[
            pltpu.VMEM((16, 16, 128), F32),
            pltpu.VMEM((16, 16, 128), F32),
            pltpu.SMEM((1, 1), F32),
            pltpu.VMEM((2, 16, 16), jnp.int32),
            pltpu.SMEM((1, 1), jnp.int32),
            pltpu.VMEM((64, 16, 16, 128), BF16),
            pltpu.VMEM((1024, 1024), F32),
            pltpu.VMEM((16, 128), F32),
            pltpu.VMEM((16, 128), F32),
            pltpu.VMEM((4, 16, 128), F32),
            pltpu.VMEM((16, 16, 128), F32),
            pltpu.VMEM((64, 2048), BF16),
            pltpu.VMEM((32, 256), BF16),
            pltpu.VMEM((16, 2048), BF16),
            pltpu.VMEM((128, 2048), BF16),
            pltpu.VMEM((1152, 128), BF16),
            pltpu.VMEM((128, 1024), BF16),
            pltpu.VMEM((8, 128), F32),
            pltpu.VMEM((8, 128), F32),
            pltpu.VMEM((16, 3, 128), F32),
            pltpu.VMEM((16, 33, 128), F32),
            pltpu.SemaphoreType.DMA((6,)),
            pltpu.SemaphoreType.DMA((8,)),
            pltpu.SemaphoreType.DMA((4,)),
            pltpu.SemaphoreType.DMA((4,)),
            pltpu.SemaphoreType.DMA((15,)),
            pltpu.SemaphoreType.DMA((15,)),
            pltpu.SemaphoreType.DMA((15,)),
            pltpu.SemaphoreType.DMA((15,)),
        ],
        compiler_params=pltpu.CompilerParams(
            collective_id=0, has_side_effects=True, vmem_limit_bytes=62 * 1024 * 1024
        ),
    )(residual, direction, rz_old.reshape(1, 1), wall_flags, owner_list.reshape(1, 1), coarse_basis, coarse_inverse)
    return solution + step * direction, residual - step * applied, precond + ratio * direction


def solution(mesh):
    field = P("stream", "span", None)
    in_specs = (
        field,
        field,
        field,
        P(),
        P(None, "stream", "span"),
        P(("stream", "span")),
        P(None, "stream", "span", None),
        P(),
    )
    return jax.shard_map(
        on_device, mesh=mesh, in_specs=in_specs, out_specs=(field, field, field), check_vma=False
    )
```

```python
import jax
import jax.numpy as jnp
from jax import lax
from jax.experimental import pallas as pl
from jax.experimental.pallas import tpu as pltpu
from jax.sharding import PartitionSpec as P

MESH = pl.DeviceIdType.MESH
F32 = jnp.float32
BF16 = jnp.bfloat16
NT = (((1,), (1,)), ((), ()))


def iota(shape, dim):
    return lax.broadcasted_iota(jnp.int32, shape, dim)


def split3(value):
    first = value.astype(BF16)
    rest = value - first.astype(F32)
    second = rest.astype(BF16)
    third = (rest - second.astype(F32)).astype(BF16)
    return first, second, third


def places():
    stream, z = lax.axis_index("stream"), lax.axis_index("span")
    y, x, core = stream // 8, lax.rem(stream // 2, 4), lax.rem(stream, 2)
    halo = [
        (lax.rem(stream + 1, 32), z),
        (lax.rem(stream + 31, 32), z),
        (stream, lax.rem(z + 1, 8)),
        (stream, lax.rem(z + 7, 8)),
    ]
    line = [
        ((y * 4 + x) * 2 + lax.rem(core + other, 2), lax.rem(z + away, 8))
        for away in (4, 3, 5, 2, 6, 1, 7, 0)
        for other in range(2)
        if away or other
    ]
    plane = [
        ((lax.rem(y + away // 4, 4) * 4 + lax.rem(x + away % 4, 4)) * 2 + core, z)
        for away in (10, 9, 11, 6, 14, 2, 8, 5, 7, 13, 15, 1, 3, 4, 12)
    ]
    return halo, line, plane, z * 2 + core, y * 4 + x, z


def kernel(
    res_hbm, dir_hbm, rz_hbm, wall_hbm, own_hbm, basis_hbm, inv_hbm,
    app, precond, step_row, ratio_row,
    res, dirn, rz, wall, own, basis, inv,
    low_face, high_face, halo_buf, inv_diag, w_all, w_faces, w_rows, edge, group_sum, per_cell, early, v_ref,
    line_buf, plane_buf,
    in_sem, basis_sem, halo_send, halo_recv, line_send, line_recv, plane_send, plane_recv,
):
    halo, line, plane, line_me, plane_me, z = places()
    loads = [
        pltpu.make_async_copy(src, dst, in_sem.at[i])
        for i, (src, dst) in enumerate(
            ((dir_hbm, dirn), (wall_hbm, wall), (res_hbm, res), (rz_hbm, rz), (own_hbm, own), (inv_hbm, inv))
        )
    ]
    loads[0].start()
    barrier = pltpu.get_barrier_semaphore()
    for peer in line[:2] + plane[:1] + line[2:6] + plane[1:5] + halo[:2] + line[6:10] + plane[5:] + line[10:] + halo[2:]:
        pl.semaphore_signal(barrier, inc=1, device_id=peer, device_id_type=MESH)
    basis_loads = [
        pltpu.make_async_copy(basis_hbm.at[pl.ds(8 * i, 8)], basis.at[pl.ds(8 * i, 8)], basis_sem.at[i])
        for i in range(8)
    ]
    for load in loads[1:5] + basis_loads + loads[5:]:
        load.start()

    lane = iota((16, 128), 1)
    row = iota((16, 128), 0)
    group_sum[0:1024, :] = (iota((1024, 128), 0) // 16 == iota((1024, 128), 1) % 64).astype(F32).astype(BF16)
    group_sum[1024:1152, :] = (iota((128, 128), 0) // 2 == iota((128, 128), 1) % 64).astype(F32).astype(BF16)
    per_cell[...] = (iota((128, 1024), 0) % 64 == iota((128, 1024), 1) // 16).astype(F32).astype(BF16)

    loads[0].wait()
    for x in range(16):
        low_face[pl.ds(x, 1), :] = dirn[x, pl.ds(0, 1), :]
        high_face[pl.ds(x, 1), :] = dirn[x, pl.ds(15, 1), :]
    loads[1].wait()
    loads[2].wait()
    same = iota((16, 16), 0) == iota((16, 16), 1)
    keep_low = (1 - wall[0]).astype(F32)
    keep_top = (1 - wall[1]).astype(F32)
    sum_rr = jnp.zeros((16, 128), F32)
    for x in range(16):
        own_d = dirn[x]
        low = jnp.sum(jnp.where(same, keep_low[x : x + 1, :], 0.0), axis=1, keepdims=True)
        top = jnp.sum(jnp.where(same, keep_top[x : x + 1, :], 0.0), axis=1, keepdims=True)
        around = jnp.where(lane == 0, own_d * low, pltpu.roll(own_d, 1, 1))
        around += jnp.where(lane == 127, own_d * top, pltpu.roll(own_d, 127, 1))
        around += jnp.where(row == 0, 0.0, pltpu.roll(own_d, 1, 0))
        around += jnp.where(row == 15, 0.0, pltpu.roll(own_d, 15, 0))
        if x > 0:
            around += dirn[x - 1]
        if x < 15:
            around += dirn[x + 1]
        app[x] = 6.0 * own_d - around
        diag = 6.0 - jnp.where(lane == 0, low, 0.0) - jnp.where(lane == 127, top, 0.0)
        inverse = 1.0 / diag
        inv_diag[x] = inverse
        r = res[x]
        sum_rr += r * r * inverse
        r_low = r.astype(BF16)
        at = slice(128 * x, 128 * x + 128)
        w_all[0:16, at] = r_low
        w_all[16:32, at] = (r - r_low.astype(F32)).astype(BF16)
        if 0 < x < 15:
            inner = jnp.where((row > 0) & (row < 15), app[x], 0.0)
        else:
            inner = jnp.zeros((16, 128), F32)
            w_rows[:, at] = inner.astype(BF16)
        q_low = inner.astype(BF16)
        w_all[32:48, at] = q_low
        w_all[48:64, at] = (inner - q_low.astype(F32)).astype(BF16)

    pl.semaphore_wait(barrier, len(halo + line + plane))
    sends = []
    for i, (src, peer) in enumerate(zip((dirn.at[15], dirn.at[0], high_face, low_face), halo)):
        copy = pltpu.make_async_remote_copy(
            src_ref=src, dst_ref=halo_buf.at[i], send_sem=halo_send.at[i], recv_sem=halo_recv.at[i],
            device_id=peer, device_id_type=MESH,
        )
        copy.start()
        sends.append(copy)

    pick = iota((64, 1024), 0) % 16 == iota((64, 1024), 1) % 16

    def slab(low, high):
        return jnp.concatenate([basis[:, low].reshape(1024, 128), basis[:, high].reshape(1024, 128)], axis=1)

    def picked(total):
        total = jnp.where(pick[0 : total.shape[0]], total, 0.0)
        return [jnp.sum(total[16 * i : 16 * i + 16], axis=0, keepdims=True) for i in range(total.shape[0] // 16)]

    def stack(lines):
        at = iota((8, lines[0].shape[1]), 0)
        total = jnp.zeros(at.shape, F32)
        for i, line in enumerate(lines):
            total = jnp.where(at == i, line, total)
        return total

    def by_basis(both, groups):
        one, two, three = (part.astype(F32) for part in split3(both))
        stacked = jnp.concatenate([one, two, three, jnp.zeros_like(one)], axis=0).astype(BF16)
        sums = jnp.dot(stacked, groups, preferred_element_type=F32)
        return sums[0:8] + sums[8:16] + sums[16:24]

    for load in basis_loads:
        load.wait()
    total = jnp.zeros((64, 1024), F32)
    for pair in range(8):
        total += lax.dot_general(
            w_all[:, 256 * pair : 256 * pair + 256], slab(2 * pair, 2 * pair + 1), NT, preferred_element_type=F32
        )
    early[...] = by_basis(stack(picked(total)), group_sum[0:1024, :])
    choose = (
        (iota((32, 256), 0) // 2 == iota((32, 256), 1) // 16)
        & (iota((32, 256), 1) % 16 == 15 * (iota((32, 256), 0) % 2))
    ).astype(F32).astype(BF16)
    for part in range(4):
        for pair in range(8):
            tile = jnp.concatenate(
                [basis[16 * part : 16 * part + 16, 2 * pair + i].reshape(256, 128) for i in range(2)], axis=1
            )
            edge[32 * part : 32 * part + 32, 256 * pair : 256 * pair + 256] = jnp.dot(
                choose, tile, preferred_element_type=F32
            ).astype(BF16)

    for copy in sends:
        copy.wait_recv()
    from_low = jnp.where(z > 0, 1.0, 0.0)
    from_high = jnp.where(z < 7, 1.0, 0.0)
    sum_dq = jnp.zeros((16, 128), F32)
    sum_rq = jnp.zeros((16, 128), F32)
    sum_qq = jnp.zeros((16, 128), F32)
    for x in range(16):
        q = app[x]
        if x == 0:
            q -= halo_buf[0]
        if x == 15:
            q -= halo_buf[1]
        q -= jnp.where(row == 0, halo_buf[2, pl.ds(x, 1), :] * from_low, 0.0)
        q -= jnp.where(row == 15, halo_buf[3, pl.ds(x, 1), :] * from_high, 0.0)
        app[x] = q
        scaled = q * inv_diag[x]
        sum_dq += dirn[x] * q
        sum_rq += res[x] * scaled
        sum_qq += q * scaled
        q_low = q.astype(BF16)
        q_rest = q - q_low.astype(F32)
        if x in (0, 15):
            at = slice(0, 128) if x == 0 else slice(128, 256)
            w_faces[0:16, at] = q_low
            w_faces[16:32, at] = q_rest.astype(BF16)
        else:
            q_low = q_low.astype(F32)
            ends = jnp.where(row == 0, q_low[0:1], jnp.where(row == 1, q_low[15:16], 0.0))
            ends = jnp.where(row == 2, q_rest[0:1], jnp.where(row == 3, q_rest[15:16], ends))
            w_rows[:, 128 * x : 128 * x + 128] = ends.astype(BF16)
    faces = picked(lax.dot_general(w_faces[...], slab(0, 15), NT, preferred_element_type=F32))
    ends = lax.dot_general(w_rows[...], edge[...], NT, preferred_element_type=F32)
    ends = jnp.where(row % 2 == lane % 2, ends, 0.0)
    late = by_basis(
        jnp.concatenate([stack(faces), stack([ends[0:1] + ends[1:2], ends[2:3] + ends[3:4]])], axis=1), group_sum[...]
    )
    part_res = early[...]
    part_app = part_res[2:4] + late[0:2]
    loads[4].wait()
    lane1 = lane[0:1]
    scalars = jnp.zeros((1, 128), F32)
    for i, value in enumerate((sum_dq, sum_rr, sum_rq, sum_qq)):
        whole = jnp.sum(jnp.sum(value, axis=0, keepdims=True), axis=1, keepdims=True)
        scalars = jnp.where(lane1 == i, whole, scalars)
    line_buf[line_me, pl.ds(0, 1), :] = jnp.where(lane1 < 64, part_res[0:1, :], part_app[0:1, :])
    line_buf[line_me, pl.ds(1, 1), :] = jnp.where(lane1 < 64, part_res[1:2, :], part_app[1:2, :])
    line_buf[line_me, pl.ds(2, 1), :] = scalars
    spot = lax.rem(plane_me, 8) * 16 + line_me
    line_buf[line_me, pl.ds(3, 1), :] = own[0, 0].astype(F32) * jnp.where(lane1 == spot, 1.0, 0.0)

    copies = []
    for i, peer in enumerate(line):
        copy = pltpu.make_async_remote_copy(
            src_ref=line_buf.at[line_me], dst_ref=line_buf.at[line_me], send_sem=line_send.at[i],
            recv_sem=line_recv.at[i], device_id=peer, device_id_type=MESH,
        )
        copy.start()
        copies.append(copy)
    sends += copies
    for copy in copies:
        copy.wait_recv()
    for kind in range(2):
        plane_buf[plane_me, pl.ds(16 * kind, 16), :] = line_buf[:, kind, :]
    for kind in range(2, 4):
        plane_buf[plane_me, pl.ds(30 + kind, 1), :] = jnp.sum(line_buf[:, kind, :], axis=0, keepdims=True)
    copies = []
    for i, peer in enumerate(plane):
        copy = pltpu.make_async_remote_copy(
            src_ref=plane_buf.at[plane_me], dst_ref=plane_buf.at[plane_me], send_sem=plane_send.at[i],
            recv_sem=plane_recv.at[i], device_id=peer, device_id_type=MESH,
        )
        copy.start()
        copies.append(copy)
    sends += copies
    loads[3].wait()
    loads[5].wait()
    for copy in copies:
        copy.wait_recv()

    scalars = plane_buf[:, 32, :]
    totals = jnp.sum(scalars, axis=0, keepdims=True)
    rz_old = rz[0, 0]
    step = rz_old / totals[:, 0:1]
    step_row[0] = jnp.broadcast_to(step, (1, 128))
    owners = plane_buf[:, 33, :]
    owners = jnp.concatenate([jnp.sum(owners[8 * i : 8 * i + 8], axis=0, keepdims=True) for i in range(2)], axis=1)
    at = iota((16, 256), 0)
    wanted = jnp.where(at < 8, 2 * at, 2 * at - 15).astype(F32)
    chosen = (owners == wanted).astype(F32).astype(BF16)
    sums = jnp.zeros((16, 256), F32)
    for part in split3(jnp.concatenate([plane_buf[:, 0:16].reshape(256, 128), plane_buf[:, 16:32].reshape(256, 128)], axis=1)):
        sums += jnp.dot(chosen, part, preferred_element_type=F32)
    lane8 = iota((8, 128), 1)
    row8 = iota((8, 128), 0)

    def coarse(even, odd):
        return jnp.where(
            lane8 < 64, even - step * pltpu.roll(even, 64, 1), pltpu.roll(odd, 64, 1) - step * odd
        )

    rhs = coarse(sums[0:8, 0:128], sums[8:16, 0:128])
    rhs_rest = coarse(sums[0:8, 128:256], sums[8:16, 128:256])
    v_ref[...] = rhs

    def block(tile, total):
        values = v_ref[pl.ds(tile, 1), :]
        for k in range(16):
            column = jnp.sum(jnp.where(lane8 == row8 + 8 * k, values, 0.0), axis=1, keepdims=True)
            total += column * inv[pl.ds(pl.multiple_of(tile * 128 + 8 * k, 8), 8), :]
        return total

    total = lax.fori_loop(0, 8, block, jnp.zeros((8, 1024), F32), unroll=True)
    answer = jnp.zeros((8, 128), F32)
    for tile in range(8):
        answer = jnp.where(
            row8 == tile, jnp.sum(total[:, 128 * tile : 128 * tile + 128], axis=0, keepdims=True), answer
        )
    answer = answer.astype(BF16).astype(F32)
    inner = jnp.sum(jnp.sum(answer * (rhs + rhs_rest), axis=0, keepdims=True), axis=1, keepdims=True)
    rz_new = totals[:, 1:2] - 2.0 * step * totals[:, 2:3] + step * step * totals[:, 3:4] + inner
    ratio = rz_new / rz_old
    ratio_row[0] = jnp.broadcast_to(ratio, (1, 128))
    mine = own[0, 0]
    here = jnp.where(row8 == (mine >> 1), jnp.where((lane8 >> 6) == (mine & 1), answer, 0.0), 0.0)
    here = jnp.broadcast_to(jnp.sum(here, axis=0, keepdims=True), (16, 128)).astype(BF16)
    spread = jnp.dot(here, per_cell[...], preferred_element_type=F32)
    spread = jnp.where(pick[0:16], spread, 0.0).astype(BF16)
    for pair in range(8):
        correction = jnp.dot(spread, slab(2 * pair, 2 * pair + 1), preferred_element_type=F32)
        for side in range(2):
            x = 2 * pair + side
            updated = res[x] - step * app[x]
            precond[x] = updated * inv_diag[x] + correction[:, 128 * side : 128 * side + 128]
    for copy in sends:
        copy.wait_send()


def on_device(solution, residual, direction, rz_old, wall_flags, owner_list, coarse_basis, coarse_inverse):
    block = pltpu.VMEM((16, 16, 128), F32)
    line = pltpu.VMEM((1, 1, 128), F32)
    applied, precond, step, ratio = pl.pallas_call(
        kernel,
        out_shape=(block, block, line, line),
        in_specs=[pl.BlockSpec(memory_space=pltpu.HBM)] * 7,
        out_specs=(pl.BlockSpec(memory_space=pltpu.VMEM),) * 4,
        scratch_shapes=[
            pltpu.VMEM((16, 16, 128), F32),
            pltpu.VMEM((16, 16, 128), F32),
            pltpu.SMEM((1, 1), F32),
            pltpu.VMEM((2, 16, 16), jnp.int32),
            pltpu.SMEM((1, 1), jnp.int32),
            pltpu.VMEM((64, 16, 16, 128), BF16),
            pltpu.VMEM((1024, 1024), F32),
            pltpu.VMEM((16, 128), F32),
            pltpu.VMEM((16, 128), F32),
            pltpu.VMEM((4, 16, 128), F32),
            pltpu.VMEM((16, 16, 128), F32),
            pltpu.VMEM((64, 2048), BF16),
            pltpu.VMEM((32, 256), BF16),
            pltpu.VMEM((16, 2048), BF16),
            pltpu.VMEM((128, 2048), BF16),
            pltpu.VMEM((1152, 128), BF16),
            pltpu.VMEM((128, 1024), BF16),
            pltpu.VMEM((8, 128), F32),
            pltpu.VMEM((8, 128), F32),
            pltpu.VMEM((16, 4, 128), F32),
            pltpu.VMEM((16, 34, 128), F32),
            pltpu.SemaphoreType.DMA((6,)),
            pltpu.SemaphoreType.DMA((8,)),
            pltpu.SemaphoreType.DMA((4,)),
            pltpu.SemaphoreType.DMA((4,)),
            pltpu.SemaphoreType.DMA((15,)),
            pltpu.SemaphoreType.DMA((15,)),
            pltpu.SemaphoreType.DMA((15,)),
            pltpu.SemaphoreType.DMA((15,)),
        ],
        compiler_params=pltpu.CompilerParams(
            collective_id=0, has_side_effects=True, vmem_limit_bytes=62 * 1024 * 1024
        ),
    )(residual, direction, rz_old.reshape(1, 1), wall_flags, owner_list.reshape(1, 1), coarse_basis, coarse_inverse)
    return solution + step * direction, residual - step * applied, precond + ratio * direction


def solution(mesh):
    field = P("stream", "span", None)
    in_specs = (
        field,
        field,
        field,
        P(),
        P(None, "stream", "span"),
        P(("stream", "span")),
        P(None, "stream", "span", None),
        P(),
    )
    return jax.shard_map(
        on_device, mesh=mesh, in_specs=in_specs, out_specs=(field, field, field), check_vma=False
    )
```

```python
import jax
import jax.numpy as jnp
from jax import lax
from jax.experimental import pallas as pl
from jax.experimental.pallas import tpu as pltpu
from jax.sharding import PartitionSpec as P

MESH = pl.DeviceIdType.MESH
F32 = jnp.float32
BF16 = jnp.bfloat16
NT = (((1,), (1,)), ((), ()))


def iota(shape, dim):
    return lax.broadcasted_iota(jnp.int32, shape, dim)


def split3(value):
    first = value.astype(BF16)
    rest = value - first.astype(F32)
    second = rest.astype(BF16)
    third = (rest - second.astype(F32)).astype(BF16)
    return first, second, third


def places():
    stream, z = lax.axis_index("stream"), lax.axis_index("span")
    y, x, core = stream // 8, lax.rem(stream // 2, 4), lax.rem(stream, 2)
    halo = [
        (lax.rem(stream + 1, 32), z),
        (lax.rem(stream + 31, 32), z),
        (stream, lax.rem(z + 1, 8)),
        (stream, lax.rem(z + 7, 8)),
    ]
    line = [
        ((y * 4 + x) * 2 + lax.rem(core + other, 2), lax.rem(z + away, 8))
        for away in (4, 3, 5, 2, 6, 1, 7, 0)
        for other in range(2)
        if away or other
    ]
    plane = [
        ((lax.rem(y + away // 4, 4) * 4 + lax.rem(x + away % 4, 4)) * 2 + core, z)
        for away in (10, 9, 11, 6, 14, 2, 8, 5, 7, 13, 15, 1, 3, 4, 12)
    ]
    return halo, line, plane, z * 2 + core, y * 4 + x, z


def kernel(
    res_hbm, dir_hbm, rz_hbm, wall_hbm, own_hbm, basis_hbm, inv_hbm,
    app, precond, step_row, ratio_row,
    res, dirn, rz, wall, own, basis, inv,
    low_face, high_face, halo_buf, inv_diag, w_all, w_faces, w_rows, edge, group_sum, per_cell, early, v_ref,
    line_buf, plane_buf,
    in_sem, basis_sem, halo_send, halo_recv, line_send, line_recv, plane_send, plane_recv,
):
    halo, line, plane, line_me, plane_me, z = places()
    loads = [
        pltpu.make_async_copy(src, dst, in_sem.at[i])
        for i, (src, dst) in enumerate(
            ((dir_hbm, dirn), (wall_hbm, wall), (res_hbm, res), (rz_hbm, rz), (own_hbm, own), (inv_hbm, inv))
        )
    ]
    loads[0].start()
    barrier = pltpu.get_barrier_semaphore()
    stream = lax.axis_index("stream")
    beside = [(lax.rem(stream + 31 + 2 * lax.rem(stream, 2), 32), z)]
    greeted = line[:2] + plane[:1] + line[2:6] + plane[1:5] + beside + line[6:10] + plane[5:] + line[10:]
    for peer in greeted:
        pl.semaphore_signal(barrier, inc=1, device_id=peer, device_id_type=MESH)
    basis_loads = [
        pltpu.make_async_copy(basis_hbm.at[pl.ds(8 * i, 8)], basis.at[pl.ds(8 * i, 8)], basis_sem.at[i])
        for i in range(8)
    ]
    for load in loads[1:5] + basis_loads + loads[5:]:
        load.start()

    lane = iota((16, 128), 1)
    row = iota((16, 128), 0)
    group_sum[0:1024, :] = (iota((1024, 128), 0) // 16 == iota((1024, 128), 1) % 64).astype(F32).astype(BF16)
    group_sum[1024:1152, :] = (iota((128, 128), 0) // 2 == iota((128, 128), 1) % 64).astype(F32).astype(BF16)
    per_cell[...] = (iota((128, 1024), 0) % 64 == iota((128, 1024), 1) // 16).astype(F32).astype(BF16)

    loads[0].wait()
    for x in range(16):
        low_face[pl.ds(x, 1), :] = dirn[x, pl.ds(0, 1), :]
        high_face[pl.ds(x, 1), :] = dirn[x, pl.ds(15, 1), :]
    loads[1].wait()
    loads[2].wait()
    same = iota((16, 16), 0) == iota((16, 16), 1)
    keep_low = (1 - wall[0]).astype(F32)
    keep_top = (1 - wall[1]).astype(F32)
    sum_rr = jnp.zeros((16, 128), F32)
    for x in range(16):
        own_d = dirn[x]
        low = jnp.sum(jnp.where(same, keep_low[x : x + 1, :], 0.0), axis=1, keepdims=True)
        top = jnp.sum(jnp.where(same, keep_top[x : x + 1, :], 0.0), axis=1, keepdims=True)
        around = jnp.where(lane == 0, own_d * low, pltpu.roll(own_d, 1, 1))
        around += jnp.where(lane == 127, own_d * top, pltpu.roll(own_d, 127, 1))
        around += jnp.where(row == 0, 0.0, pltpu.roll(own_d, 1, 0))
        around += jnp.where(row == 15, 0.0, pltpu.roll(own_d, 15, 0))
        if x > 0:
            around += dirn[x - 1]
        if x < 15:
            around += dirn[x + 1]
        app[x] = 6.0 * own_d - around
        diag = 6.0 - jnp.where(lane == 0, low, 0.0) - jnp.where(lane == 127, top, 0.0)
        inverse = 1.0 / diag
        inv_diag[x] = inverse
        r = res[x]
        sum_rr += r * r * inverse
        r_low = r.astype(BF16)
        at = slice(128 * x, 128 * x + 128)
        w_all[0:16, at] = r_low
        w_all[16:32, at] = (r - r_low.astype(F32)).astype(BF16)
        if 0 < x < 15:
            inner = jnp.where((row > 0) & (row < 15), app[x], 0.0)
        else:
            inner = jnp.zeros((16, 128), F32)
            w_rows[:, at] = inner.astype(BF16)
        q_low = inner.astype(BF16)
        w_all[32:48, at] = q_low
        w_all[48:64, at] = (inner - q_low.astype(F32)).astype(BF16)

    pl.semaphore_wait(barrier, len(greeted))
    sends = []
    for i, (src, peer) in enumerate(zip((dirn.at[15], dirn.at[0], high_face, low_face), halo)):
        copy = pltpu.make_async_remote_copy(
            src_ref=src, dst_ref=halo_buf.at[i], send_sem=halo_send.at[i], recv_sem=halo_recv.at[i],
            device_id=peer, device_id_type=MESH,
        )
        copy.start()
        sends.append(copy)

    pick = iota((64, 1024), 0) % 16 == iota((64, 1024), 1) % 16

    def slab(low, high):
        return jnp.concatenate([basis[:, low].reshape(1024, 128), basis[:, high].reshape(1024, 128)], axis=1)

    def picked(total):
        total = jnp.where(pick[0 : total.shape[0]], total, 0.0)
        return [jnp.sum(total[16 * i : 16 * i + 16], axis=0, keepdims=True) for i in range(total.shape[0] // 16)]

    def stack(lines):
        at = iota((8, lines[0].shape[1]), 0)
        total = jnp.zeros(at.shape, F32)
        for i, line in enumerate(lines):
            total = jnp.where(at == i, line, total)
        return total

    def by_basis(both, groups):
        one, two, three = (part.astype(F32) for part in split3(both))
        stacked = jnp.concatenate([one, two, three, jnp.zeros_like(one)], axis=0).astype(BF16)
        sums = jnp.dot(stacked, groups, preferred_element_type=F32)
        return sums[0:8] + sums[8:16] + sums[16:24]

    for load in basis_loads:
        load.wait()
    total = jnp.zeros((64, 1024), F32)
    for pair in range(8):
        total += lax.dot_general(
            w_all[:, 256 * pair : 256 * pair + 256], slab(2 * pair, 2 * pair + 1), NT, preferred_element_type=F32
        )
    early[...] = by_basis(stack(picked(total)), group_sum[0:1024, :])
    choose = (
        (iota((32, 256), 0) // 2 == iota((32, 256), 1) // 16)
        & (iota((32, 256), 1) % 16 == 15 * (iota((32, 256), 0) % 2))
    ).astype(F32).astype(BF16)
    for part in range(4):
        for pair in range(8):
            tile = jnp.concatenate(
                [basis[16 * part : 16 * part + 16, 2 * pair + i].reshape(256, 128) for i in range(2)], axis=1
            )
            edge[32 * part : 32 * part + 32, 256 * pair : 256 * pair + 256] = jnp.dot(
                choose, tile, preferred_element_type=F32
            ).astype(BF16)

    for copy in sends:
        copy.wait_recv()
    from_low = jnp.where(z > 0, 1.0, 0.0)
    from_high = jnp.where(z < 7, 1.0, 0.0)
    sum_dq = jnp.zeros((16, 128), F32)
    sum_rq = jnp.zeros((16, 128), F32)
    sum_qq = jnp.zeros((16, 128), F32)
    for x in range(16):
        q = app[x]
        if x == 0:
            q -= halo_buf[0]
        if x == 15:
            q -= halo_buf[1]
        q -= jnp.where(row == 0, halo_buf[2, pl.ds(x, 1), :] * from_low, 0.0)
        q -= jnp.where(row == 15, halo_buf[3, pl.ds(x, 1), :] * from_high, 0.0)
        app[x] = q
        scaled = q * inv_diag[x]
        sum_dq += dirn[x] * q
        sum_rq += res[x] * scaled
        sum_qq += q * scaled
        q_low = q.astype(BF16)
        q_rest = q - q_low.astype(F32)
        if x in (0, 15):
            at = slice(0, 128) if x == 0 else slice(128, 256)
            w_faces[0:16, at] = q_low
            w_faces[16:32, at] = q_rest.astype(BF16)
        else:
            q_low = q_low.astype(F32)
            ends = jnp.where(row == 0, q_low[0:1], jnp.where(row == 1, q_low[15:16], 0.0))
            ends = jnp.where(row == 2, q_rest[0:1], jnp.where(row == 3, q_rest[15:16], ends))
            w_rows[:, 128 * x : 128 * x + 128] = ends.astype(BF16)
    faces = picked(lax.dot_general(w_faces[...], slab(0, 15), NT, preferred_element_type=F32))
    ends = lax.dot_general(w_rows[...], edge[...], NT, preferred_element_type=F32)
    ends = jnp.where(row % 2 == lane % 2, ends, 0.0)
    late = by_basis(
        jnp.concatenate([stack(faces), stack([ends[0:1] + ends[1:2], ends[2:3] + ends[3:4]])], axis=1), group_sum[...]
    )
    part_res = early[...]
    part_app = part_res[2:4] + late[0:2]
    loads[4].wait()
    lane1 = lane[0:1]
    scalars = jnp.zeros((1, 128), F32)
    for i, value in enumerate((sum_dq, sum_rr, sum_rq, sum_qq)):
        whole = jnp.sum(jnp.sum(value, axis=0, keepdims=True), axis=1, keepdims=True)
        scalars = jnp.where(lane1 == i, whole, scalars)
    line_buf[line_me, pl.ds(0, 1), :] = jnp.where(lane1 < 64, part_res[0:1, :], part_app[0:1, :])
    line_buf[line_me, pl.ds(1, 1), :] = jnp.where(lane1 < 64, part_res[1:2, :], part_app[1:2, :])
    line_buf[line_me, pl.ds(2, 1), :] = scalars
    spot = lax.rem(plane_me, 8) * 16 + line_me
    line_buf[line_me, pl.ds(3, 1), :] = own[0, 0].astype(F32) * jnp.where(lane1 == spot, 1.0, 0.0)

    copies = []
    for i, peer in enumerate(line):
        copy = pltpu.make_async_remote_copy(
            src_ref=line_buf.at[line_me], dst_ref=line_buf.at[line_me], send_sem=line_send.at[i],
            recv_sem=line_recv.at[i], device_id=peer, device_id_type=MESH,
        )
        copy.start()
        copies.append(copy)
    sends += copies
    for copy in copies:
        copy.wait_recv()
    for kind in range(2):
        plane_buf[plane_me, pl.ds(16 * kind, 16), :] = line_buf[:, kind, :]
    for kind in range(2, 4):
        plane_buf[plane_me, pl.ds(30 + kind, 1), :] = jnp.sum(line_buf[:, kind, :], axis=0, keepdims=True)
    copies = []
    for i, peer in enumerate(plane):
        copy = pltpu.make_async_remote_copy(
            src_ref=plane_buf.at[plane_me], dst_ref=plane_buf.at[plane_me], send_sem=plane_send.at[i],
            recv_sem=plane_recv.at[i], device_id=peer, device_id_type=MESH,
        )
        copy.start()
        copies.append(copy)
    sends += copies
    loads[3].wait()
    loads[5].wait()
    for copy in copies:
        copy.wait_recv()

    scalars = plane_buf[:, 32, :]
    totals = jnp.sum(scalars, axis=0, keepdims=True)
    rz_old = rz[0, 0]
    step = rz_old / totals[:, 0:1]
    step_row[0] = jnp.broadcast_to(step, (1, 128))
    owners = plane_buf[:, 33, :]
    owners = jnp.concatenate([jnp.sum(owners[8 * i : 8 * i + 8], axis=0, keepdims=True) for i in range(2)], axis=1)
    at = iota((16, 256), 0)
    wanted = jnp.where(at < 8, 2 * at, 2 * at - 15).astype(F32)
    chosen = (owners == wanted).astype(F32).astype(BF16)
    sums = jnp.zeros((16, 256), F32)
    for part in split3(jnp.concatenate([plane_buf[:, 0:16].reshape(256, 128), plane_buf[:, 16:32].reshape(256, 128)], axis=1)):
        sums += jnp.dot(chosen, part, preferred_element_type=F32)
    lane8 = iota((8, 128), 1)
    row8 = iota((8, 128), 0)

    def coarse(even, odd):
        return jnp.where(
            lane8 < 64, even - step * pltpu.roll(even, 64, 1), pltpu.roll(odd, 64, 1) - step * odd
        )

    rhs = coarse(sums[0:8, 0:128], sums[8:16, 0:128])
    rhs_rest = coarse(sums[0:8, 128:256], sums[8:16, 128:256])
    v_ref[...] = rhs

    def block(tile, total):
        values = v_ref[pl.ds(tile, 1), :]
        for k in range(16):
            column = jnp.sum(jnp.where(lane8 == row8 + 8 * k, values, 0.0), axis=1, keepdims=True)
            total += column * inv[pl.ds(pl.multiple_of(tile * 128 + 8 * k, 8), 8), :]
        return total

    total = lax.fori_loop(0, 8, block, jnp.zeros((8, 1024), F32), unroll=True)
    answer = jnp.zeros((8, 128), F32)
    for tile in range(8):
        answer = jnp.where(
            row8 == tile, jnp.sum(total[:, 128 * tile : 128 * tile + 128], axis=0, keepdims=True), answer
        )
    answer = answer.astype(BF16).astype(F32)
    inner = jnp.sum(jnp.sum(answer * (rhs + rhs_rest), axis=0, keepdims=True), axis=1, keepdims=True)
    rz_new = totals[:, 1:2] - 2.0 * step * totals[:, 2:3] + step * step * totals[:, 3:4] + inner
    ratio = rz_new / rz_old
    ratio_row[0] = jnp.broadcast_to(ratio, (1, 128))
    mine = own[0, 0]
    here = jnp.where(row8 == (mine >> 1), jnp.where((lane8 >> 6) == (mine & 1), answer, 0.0), 0.0)
    here = jnp.broadcast_to(jnp.sum(here, axis=0, keepdims=True), (16, 128)).astype(BF16)
    spread = jnp.dot(here, per_cell[...], preferred_element_type=F32)
    spread = jnp.where(pick[0:16], spread, 0.0).astype(BF16)
    for pair in range(8):
        correction = jnp.dot(spread, slab(2 * pair, 2 * pair + 1), preferred_element_type=F32)
        for side in range(2):
            x = 2 * pair + side
            updated = res[x] - step * app[x]
            precond[x] = updated * inv_diag[x] + correction[:, 128 * side : 128 * side + 128]
    for copy in sends:
        copy.wait_send()


def on_device(solution, residual, direction, rz_old, wall_flags, owner_list, coarse_basis, coarse_inverse):
    block = pltpu.VMEM((16, 16, 128), F32)
    line = pltpu.VMEM((1, 1, 128), F32)
    applied, precond, step, ratio = pl.pallas_call(
        kernel,
        out_shape=(block, block, line, line),
        in_specs=[pl.BlockSpec(memory_space=pltpu.HBM)] * 7,
        out_specs=(pl.BlockSpec(memory_space=pltpu.VMEM),) * 4,
        scratch_shapes=[
            pltpu.VMEM((16, 16, 128), F32),
            pltpu.VMEM((16, 16, 128), F32),
            pltpu.SMEM((1, 1), F32),
            pltpu.VMEM((2, 16, 16), jnp.int32),
            pltpu.SMEM((1, 1), jnp.int32),
            pltpu.VMEM((64, 16, 16, 128), BF16),
            pltpu.VMEM((1024, 1024), F32),
            pltpu.VMEM((16, 128), F32),
            pltpu.VMEM((16, 128), F32),
            pltpu.VMEM((4, 16, 128), F32),
            pltpu.VMEM((16, 16, 128), F32),
            pltpu.VMEM((64, 2048), BF16),
            pltpu.VMEM((32, 256), BF16),
            pltpu.VMEM((16, 2048), BF16),
            pltpu.VMEM((128, 2048), BF16),
            pltpu.VMEM((1152, 128), BF16),
            pltpu.VMEM((128, 1024), BF16),
            pltpu.VMEM((8, 128), F32),
            pltpu.VMEM((8, 128), F32),
            pltpu.VMEM((16, 4, 128), F32),
            pltpu.VMEM((16, 34, 128), F32),
            pltpu.SemaphoreType.DMA((6,)),
            pltpu.SemaphoreType.DMA((8,)),
            pltpu.SemaphoreType.DMA((4,)),
            pltpu.SemaphoreType.DMA((4,)),
            pltpu.SemaphoreType.DMA((15,)),
            pltpu.SemaphoreType.DMA((15,)),
            pltpu.SemaphoreType.DMA((15,)),
            pltpu.SemaphoreType.DMA((15,)),
        ],
        compiler_params=pltpu.CompilerParams(
            collective_id=0, has_side_effects=True, vmem_limit_bytes=62 * 1024 * 1024
        ),
    )(residual, direction, rz_old.reshape(1, 1), wall_flags, owner_list.reshape(1, 1), coarse_basis, coarse_inverse)
    return solution + step * direction, residual - step * applied, precond + ratio * direction


def solution(mesh):
    field = P("stream", "span", None)
    in_specs = (
        field,
        field,
        field,
        P(),
        P(None, "stream", "span"),
        P(("stream", "span")),
        P(None, "stream", "span", None),
        P(),
    )
    return jax.shard_map(
        on_device, mesh=mesh, in_specs=in_specs, out_specs=(field, field, field), check_vma=False
    )
```
